512 devices in a mesh: dp: 32 (over y, z_hi, core), tensor: 16 (over z_lo, x).
Axes of the slice: x: 4, y: 8, z: 8 (z_hi: 2, z_lo: 4; z = z_hi * 4 + z_lo), core: 2. Of those that a mesh axis runs over, the one named last changes fastest.
Arguments:
- act_in: bfloat16 [32768, 28672], P('dp', 'tensor'), may hold values from -6 to 6
- grad_out: bfloat16 [32768, 8192], P('dp', 'tensor'), may hold values from -6 to 6
- proj_in: bfloat16 [28672, 64], P('tensor'), may hold values from -0.015625 to 0.015625
- proj_out: bfloat16 [8192, 64], P('tensor'), may hold values from -0.03125 to 0.03125
- lengths: int32 [1024], P('dp'), may hold values from 1 to 32
- sources: int32 [1024], P('dp'), may hold values from 0 to 255, as said below
- val_feats: bfloat16 [128, 4096], P('dp', 'tensor'), may hold values from -0.046875 to 0.046875
- val_sets: int32 [128, 1], P('dp'), may hold values from 0 to 3
Outputs:
- source_grads: float32 [256, 4096], P('dp', 'tensor')
- pair_scores: float32 [256, 128], P('dp')
- set_scores: float32 [256, 4], P('dp')
The draws below stay inside these ranges and needn't reach their ends.
Inputs may be any that keep to these rules, and one draw needn't show every extreme that they name: The owner of source c is c // 8. Among the 32 sequences of one index of dp (aligned blocks), at most 2 have sources of one owner, and in every block some owner has exactly 2. `val_sets`: every target set holds at least one validation sequence.
All inputs are finite; a program needn't handle non-finite values.
Results may differ from the reference program's by a relative error of at most 0.0052.
Values may be sent and summed in bfloat16 or wider, within the bound.
No kernel may reach another device: no remote copies, remote signals or barrier semaphores. Data moves between devices by JAX's collectives and lax.ppermute only.
A program may use at most 64 MiB of HBM per device.

```python
import jax
import jax.numpy as jnp
from jax import lax

D = 8192
FF = 28672
PROJ = 64
SETS = 4
LEN = 32
SEQ_DEV = 32
SRC_DEV = 8
SEQS = 1024
TOKENS = 32768
SOURCES = 256
NVAL = 128
CAP = 2
N_DP = 32


def draw_block(block_key):
    first_key, second_key, third_key, fourth_key = jax.random.split(block_key, 4)
    slot_total = N_DP * CAP
    slot_owner = jnp.arange(slot_total, dtype=jnp.int32) // CAP
    ranking = jax.random.permutation(first_key, slot_total).astype(jnp.int32)
    fullest = jax.random.randint(second_key, (), 0, N_DP, dtype=jnp.int32)
    ranking = jnp.where(slot_owner == fullest, ranking - slot_total, ranking)
    chosen = jnp.argsort(ranking, stable=True)[:SEQ_DEV]
    owners = slot_owner[chosen]
    owners = owners[jax.random.permutation(third_key, SEQ_DEV)]
    within = jax.random.randint(fourth_key, (SEQ_DEV,), 0, SRC_DEV, dtype=jnp.int32)
    return owners * SRC_DEV + within


def draw_sources(key, part):
    key = jax.random.fold_in(key, 7)
    block_keys = jax.random.split(key, N_DP)
    return jax.vmap(draw_block)(block_keys).reshape(-1).astype(jnp.int32)


def set_ends(drawn, own_key, smallest, high):
    spot = [jax.random.randint(jax.random.fold_in(own_key, axis), (), 0, length) for axis, length in enumerate(drawn.shape)]
    longest = drawn.shape.index(max(drawn.shape))
    beside = spot[:longest] + [(spot[longest] + 1) % drawn.shape[longest]] + spot[longest + 1:]
    return drawn.at[tuple(spot)].set(smallest).at[tuple(beside)].set(high)


def block_scale(rng, dims, pieces, smallest, high):
    def one(dim, shards_of):
        draws = jax.random.uniform(jax.random.fold_in(jax.random.fold_in(rng, 6), dim), (shards_of,), jnp.float32, smallest / len(pieces), high / len(pieces))
        return jnp.repeat(jnp.exp(draws), dims[dim] // shards_of).reshape((-1,) + (1,) * (len(dims) - dim - 1))

    loudness = one(*pieces[0])
    for cut in pieces[1:]:
        loudness = loudness * one(*cut)
    return loudness


def distinct(key, rows, count, top, lift):
    order = jax.random.permutation(jax.random.fold_in(key, 1), count)
    favour = order
    for power in range(3):
        favour = favour * favour // count
    favour = favour * lift // count
    tickets = jax.random.randint(jax.random.fold_in(key, 2), (rows, count), 0, 4096) + favour
    sure = jax.random.permutation(jax.random.fold_in(key, 3), rows)[jnp.arange(count) % rows]
    tickets = jnp.where(jnp.arange(rows)[:, None] == sure[None, :], 1 << 14, tickets)
    score = tickets * count + jnp.arange(count)
    return lax.top_k(score.astype(jnp.int32), top)[1].astype(jnp.int32)


def bell_draw(stream_key, shape, spread, most, cuts=(), kind=jnp.bfloat16):
    array = jax.random.normal(stream_key, shape, jnp.float32) * spread
    if len(cuts) > 0:
        array = block_scale(stream_key, shape, cuts, -0.22, 0.18) * array
    return jnp.clip(array, min=-most, max=most).astype(kind)


def setup_inputs(seed: int = 0) -> dict:
    arg_keys = jax.random.split(jax.random.key(seed), 9)
    act_in = bell_draw(arg_keys[0], (TOKENS, FF), 1.0, 6.0, ((0, 32), (1, 16)))
    grad_out = bell_draw(arg_keys[1], (TOKENS, D), 1.0, 6.0, ((0, 32), (1, 16)))
    proj_in = bell_draw(arg_keys[2], (FF, PROJ), (4 * FF) ** -0.5, 0.015625, ((0, 16),))
    proj_out = bell_draw(arg_keys[3], (D, PROJ), (4 * D) ** -0.5, 0.03125, ((0, 16),))
    lengths = set_ends(jax.random.randint(arg_keys[4], (SEQS,), 1, LEN + 1), jax.random.fold_in(arg_keys[4], 1), 1, LEN).astype(jnp.int32)
    sources = draw_sources(jax.random.fold_in(arg_keys[8], 71), 0)
    val_feats = bell_draw(arg_keys[6], (NVAL, PROJ * PROJ), (1.0 / (2 * PROJ)), 0.046875, ((0, 32), (1, 16)))
    val_sets = distinct(arg_keys[7], NVAL, SETS, 1, 0)
    return {"act_in": act_in, "grad_out": grad_out, "proj_in": proj_in, "proj_out": proj_out, "lengths": lengths, "sources": sources, "val_feats": val_feats, "val_sets": val_sets}


def reference(act_in, grad_out, proj_in, proj_out, lengths, sources, val_feats, val_sets):
    seq_total = lengths.shape[0]
    in_proj = jnp.dot(act_in, proj_in, preferred_element_type=jnp.float32)
    out_proj = jnp.dot(grad_out, proj_out, preferred_element_type=jnp.float32)
    live_mask = (jnp.arange(LEN, dtype=jnp.int32)[None, :] < lengths[:, None]).astype(jnp.float32)
    in_masked = (in_proj.reshape(seq_total, LEN, PROJ) * live_mask[:, :, None]).astype(jnp.bfloat16)
    out_masked = (out_proj.reshape(seq_total, LEN, PROJ) * live_mask[:, :, None]).astype(jnp.bfloat16)
    grads = jnp.einsum("sta,stb->sab", out_masked.astype(jnp.float32), in_masked.astype(jnp.float32))
    grads = grads.reshape(seq_total, PROJ * PROJ).astype(jnp.bfloat16)
    source_hot = (sources[None, :] == jnp.arange(SOURCES, dtype=jnp.int32)[:, None]).astype(jnp.bfloat16)
    source_grads = jnp.dot(source_hot, grads, preferred_element_type=jnp.float32)
    pair_scores = jnp.dot(source_grads, val_feats.astype(jnp.float32).T, precision=lax.Precision.HIGHEST)
    set_hot = (val_sets[:, 0][:, None] == jnp.arange(SETS, dtype=jnp.int32)[None, :]).astype(jnp.float32)
    set_scores = jnp.dot(pair_scores, set_hot, precision=lax.Precision.HIGHEST) / jnp.sum(set_hot, 0)
    return source_grads, pair_scores, set_scores
```

```python
import jax
import jax.numpy as jnp
from jax import lax
from jax.sharding import Mesh, PartitionSpec as P

SETS = 4
SRC_DEV = 8
SPLIT = (8, 2, 2, 4, 4)
NAMES = ("y", "h", "c", "z", "x")
DP = ("y", "h", "c")
TENSOR = ("z", "x")
CAP = 2


def exchange(blocks, axes):
    return lax.all_to_all(blocks, axes, 0, 0, tiled=True)


def local(act_in, grad_out, proj_in, proj_out, lengths, sources, val_feats, val_sets):
    bf16, f32, i32 = jnp.bfloat16, jnp.float32, jnp.int32
    width = proj_in.shape[1]
    seqs = lengths.shape[0]
    slots = act_in.shape[0] // seqs
    ranks = lax.axis_size(TENSOR)
    halves = lax.axis_size("h")
    cores = lax.axis_size("c")
    dests = lax.axis_size(("y", "c"))
    mine = seqs // ranks
    feats = width * width // ranks
    rank = lax.axis_index(TENSOR)
    vals = val_feats.shape[0]

    part_in = jnp.dot(act_in, proj_in, preferred_element_type=f32)
    part_out = jnp.dot(grad_out, proj_out, preferred_element_type=f32)
    part = jnp.concatenate([part_in, part_out], 1).astype(bf16)
    part = exchange(part.reshape(ranks, mine * slots, 2 * width), TENSOR)
    whole = jnp.sum(part.astype(f32), 0).reshape(mine, slots, 2 * width)
    live = lax.dynamic_slice_in_dim(lengths, rank * mine, mine)
    mask = jnp.arange(slots, dtype=i32)[None, :] < live[:, None]
    whole = jnp.where(mask[:, :, None], whole, 0.0)
    grads = jnp.einsum(
        "sta,stb->sab",
        whole[:, :, width:],
        whole[:, :, :width],
        precision=lax.Precision.HIGHEST,
        preferred_element_type=f32,
    ).astype(bf16)
    grads = grads.reshape(mine, ranks, feats).transpose(1, 0, 2)

    own = jnp.concatenate([sources.astype(bf16), val_sets[:, 0].astype(bf16)])
    own = jnp.pad(own, (0, feats - own.shape[0]))[None]
    extra = jnp.concatenate([val_feats, own, jnp.zeros((1, feats), bf16)], 0)
    block = jnp.concatenate(
        [grads, jnp.broadcast_to(extra[None], (ranks,) + extra.shape)], 1
    )
    block = jnp.broadcast_to(block[None], (halves,) + block.shape)
    got = exchange(block.reshape((halves * ranks,) + block.shape[2:]), ("h",) + TENSOR)
    got = got.reshape((halves, ranks) + got.shape[1:])
    rows = got[:, :, :mine].reshape(halves * seqs, feats)
    val_rows = lax.dynamic_slice_in_dim(got, rank, 1, 1)[:, 0, mine : mine + vals]
    own_row = got[:, 0, mine + vals]
    source = own_row[:, :seqs].astype(i32)
    set_row = own_row[:, seqs : seqs + vals]

    owner = source // SRC_DEV
    within = source % SRC_DEV
    same = owner[:, :, None] == owner[:, None, :]
    earlier = jnp.arange(seqs)[None, :] < jnp.arange(seqs)[:, None]
    order = jnp.sum((same & earlier[None]).astype(i32), 2)
    dest = owner // (halves * cores) * cores + owner % cores
    slot = (dest * halves + jnp.arange(halves, dtype=i32)[:, None]) * CAP + order
    here = owner // cores % halves == lax.axis_index("h")
    slot = jnp.where(here, slot, -1).reshape(-1)
    placer = jnp.arange(dests * halves * CAP, dtype=i32)[:, None] == slot[None, :]
    packed = jnp.dot(placer.astype(bf16), rows, preferred_element_type=f32).astype(bf16)
    tag = jnp.sum(jnp.where(placer, within.reshape(-1)[None, :] + 1, 0), 1).astype(bf16)
    tag = tag.reshape(dests, 1, halves * CAP)
    packed = packed.reshape(dests, halves * CAP, feats)
    val_all = jnp.broadcast_to(
        val_rows.reshape(1, halves * vals, feats), (dests, halves * vals, feats)
    )
    set_all = jnp.broadcast_to(set_row.reshape(1, 1, -1), (dests, 1, halves * vals))
    told = jnp.concatenate([tag, set_all], 2)
    told = jnp.pad(told, ((0, 0), (0, 3), (0, feats - told.shape[2])))
    came = exchange(jnp.concatenate([packed, val_all, told], 1), ("y", "c"))
    lot = halves * CAP
    arrived = came[:, :lot].reshape(-1, feats)
    tags = came[:, lot + halves * vals, :lot].astype(f32).reshape(-1)
    wanted = (jnp.arange(SRC_DEV, dtype=i32) + 1).astype(f32)
    chooser = (tags[None, :] == wanted[:, None]).astype(bf16)
    source_grads = jnp.dot(chooser, arrived, preferred_element_type=f32)

    def by_dp(a):
        a = a.reshape((-1, cores, halves, vals) + a.shape[2:])
        return jnp.swapaxes(a, 1, 2).reshape((-1,) + a.shape[4:])

    all_val = by_dp(came[:, lot : lot + halves * vals])
    all_sets = by_dp(came[:, lot + halves * vals, lot : lot + halves * vals].astype(f32))
    partial_pair = jnp.dot(
        source_grads, all_val.astype(f32).T, precision=lax.Precision.HIGHEST
    )
    spread = jnp.broadcast_to(partial_pair[None], (ranks,) + partial_pair.shape)
    pair_scores = jnp.sum(exchange(spread, TENSOR), 0)
    set_hot = (all_sets[:, None] == jnp.arange(SETS, dtype=i32).astype(f32)[None, :]).astype(f32)
    set_scores = jnp.dot(pair_scores, set_hot, precision=lax.Precision.HIGHEST) / jnp.sum(set_hot, 0)
    return (source_grads, pair_scores, set_scores)


def solution(mesh):
    parts = Mesh(mesh.devices.reshape(SPLIT), NAMES)
    placed = (
        P(DP, TENSOR),
        P(DP, TENSOR),
        P(TENSOR, None),
        P(TENSOR, None),
        P(DP),
        P(DP),
        P(DP, TENSOR),
        P(DP, None),
    )
    return jax.shard_map(
        local,
        mesh=parts,
        in_specs=placed,
        out_specs=(P(DP, TENSOR), P(DP, None), P(DP, None)),
        check_vma=False,
    )
```

```python
import jax
import jax.numpy as jnp
from jax import lax
from jax.experimental import pallas as pl
from jax.experimental.pallas import tpu as pltpu
from jax.sharding import Mesh, PartitionSpec as P

SETS = 4
SRC_DEV = 8
SPLIT = (8, 2, 2, 4, 4)
NAMES = ("y", "h", "c", "z", "x")
DP = ("y", "h", "c")
TENSOR = ("z", "x")
HALVES, CORES, RANKS = 2, 2, 16
DESTS = 16
SEQS, SLOTS, WIDTH = 32, 32, 64
MINE = SEQS // RANKS
FEATS = WIDTH * WIDTH // RANKS
VALS = 4
NVAL = 128
CAP = 2
LOT = HALVES * CAP
NONE = 256.0
PIECES = 2
AT_SOURCE, AT_SET, AT_RANK, AT_HALF, AT_DP = SEQS, 2 * SEQS, 2 * SEQS + VALS, 2 * SEQS + VALS + 1, 2 * SEQS + VALS + 2

bf16, f32, i32 = jnp.bfloat16, jnp.float32, jnp.int32
NT = (((1,), (1,)), ((), ()))
TN = (((0,), (0,)), ((), ()))


def iota(shape, dim):
    return lax.broadcasted_iota(i32, shape, dim)


def project(act_ref, grad_ref, pin_ref, pout_ref, part_ref, act, grad, pin, pout, sems):
    rows = act.shape[0] // PIECES
    moves = [(pin_ref, pin), (pout_ref, pout)]
    for k in range(PIECES):
        cut = pl.ds(k * rows, rows)
        moves += [(act_ref.at[cut], act.at[cut]), (grad_ref.at[cut], grad.at[cut])]
    copies = [pltpu.make_async_copy(*move, sems.at[i]) for i, move in enumerate(moves)]
    for copy in copies:
        copy.start()
    copies[0].wait()
    copies[1].wait()
    for k in range(PIECES):
        cut = pl.ds(k * rows, rows)
        copies[2 + 2 * k].wait()
        copies[3 + 2 * k].wait()
        a = lax.dot_general(pin[...], act[cut, :], NT, preferred_element_type=f32)
        g = lax.dot_general(pout[...], grad[cut, :], NT, preferred_element_type=f32)
        part_ref[cut, :] = jnp.concatenate([a, g], 0).T.astype(bf16)


def gradients(ints, part_ref, val_ref, out_ref, square, tile):
    rank, half = ints[AT_RANK], ints[AT_HALF]
    whole = jnp.sum(part_ref[...].astype(f32), 0)
    flat = []
    for q in range(MINE):
        rows = whole[q * SLOTS : (q + 1) * SLOTS]
        live = iota(rows.shape, 0) < ints[rank * MINE + q]
        rows = jnp.where(live, rows, 0.0)
        square[...] = lax.dot_general(
            rows[:, WIDTH:], rows[:, :WIDTH], TN, precision=lax.Precision.HIGHEST, preferred_element_type=f32
        )
        step = WIDTH // RANKS
        lines = [square[pl.ds(r, RANKS, stride=step), :] for r in range(step)]
        flat.append(jnp.concatenate(lines, 1))

    targets = []
    lane = iota((1, FEATS), 1)
    for q in range(MINE):
        s = rank * MINE + q
        source = ints[AT_SOURCE + s]
        owner = source // SRC_DEV
        order = jnp.int32(0)
        for other in range(SEQS):
            same = (ints[AT_SOURCE + other] // SRC_DEV == owner) & (other < s)
            order = order + same.astype(i32)
        dest = owner // (HALVES * CORES) * CORES + owner % CORES
        slot = dest * 16 + half * CAP + order
        targets.append((owner // CORES % HALVES, slot, source % SRC_DEV + 1))
    sets = jnp.zeros((1, FEATS), f32)
    for r in range(VALS):
        sets = jnp.where(lane == ints[AT_DP] * VALS + r, (ints[AT_SET + r] + 1).astype(f32), sets)
    shape = (RANKS, 8, FEATS)
    row, chunk = iota(shape, 1), iota(shape, 0)
    tile[...] = jnp.zeros(tile.shape, f32)
    tile[2 : 2 + VALS, :] = val_ref[...].astype(f32)
    block = jnp.where(
        chunk == rank,
        jnp.broadcast_to(tile[...][None], shape),
        jnp.where(row == 2, jnp.broadcast_to(sets[None], shape), 0.0),
    )
    for q in range(MINE):
        block = jnp.where(row == q, jnp.broadcast_to(flat[q][:, None, :], shape), block)
    for h in range(HALVES):
        sent = block
        for q in range(MINE):
            to, slot, tag = targets[q]
            slot = jnp.where(to == h, slot, jnp.int32(NONE)).astype(f32)
            told = jnp.where(lane < 128, slot, tag.astype(f32))
            sent = jnp.where(row == 6 + q, jnp.broadcast_to(told[None], shape), sent)
        out_ref[pl.ds(h * RANKS, RANKS)] = sent.astype(bf16)


def pack(ints, got_ref, out_ref):
    rank = ints[AT_RANK]
    x = got_ref[...].astype(f32)
    row, lane = iota(x.shape, 1), iota(x.shape, 2)
    half, j = iota(x.shape, 0) // RANKS, iota(x.shape, 0) % RANKS
    over = lane % 16
    turned = pltpu.roll(x, 2, 1)
    slot = jnp.concatenate([turned[:, :, :128]] * 2, 2).astype(i32)
    told = jnp.concatenate([x[:, :, :128]] * 2, 2).astype(i32)
    val = (j == rank) & (over == LOT + half * VALS + row - 2)
    sets = (j == (rank + 1) % RANKS) & (row == 2) & (over == LOT + HALVES * VALS)
    moves = (
        ((row < 2) & (slot == lane))
        | ((row >= 6) & (told + LOT + HALVES * VALS == lane))
        | ((row >= 2) & (row < 2 + VALS) & (val | sets))
    )
    moves = jnp.where(moves, 1.0, 0.0).reshape(-1, FEATS).astype(bf16)
    x = jnp.where((row >= 6) & (lane < 128), 0.0, x).reshape(-1, FEATS).astype(bf16)
    packed = lax.dot_general(moves, x, TN, preferred_element_type=f32)
    out_ref[...] = packed.astype(bf16).reshape(out_ref.shape)


def score(came_ref, grads_ref, spread_ref, sets_ref):
    x = came_ref[...].astype(f32).reshape(-1, FEATS)
    rows = x.shape[0]
    half = x[:, :128]
    row = iota(half.shape, 0) % 16
    tags = pltpu.roll(x, rows - (LOT + HALVES * VALS), 0)[:, 128:].astype(i32)
    chooser = jnp.where((row < LOT) & (tags == iota(half.shape, 1) + 1), 1.0, 0.0).astype(bf16)
    x = x.astype(bf16)
    source_grads = lax.dot_general(chooser, x, TN, preferred_element_type=f32)[:SRC_DEV]
    grads_ref[...] = source_grads
    sets_ref[...] = jnp.broadcast_to(
        jnp.sum(jnp.where(row == LOT + HALVES * VALS, half, 0.0), 0, keepdims=True), sets_ref.shape
    )
    v, n = iota((NVAL, rows), 0), iota((NVAL, rows), 1)
    r, c, h, y = v % VALS, v // VALS % CORES, v // (VALS * CORES) % HALVES, v // (VALS * CORES * HALVES)
    pick = n == (y * CORES + c) * 16 + LOT + h * VALS + r
    val = jnp.dot(jnp.where(pick, 1.0, 0.0).astype(bf16), x, preferred_element_type=f32)
    pair = lax.dot_general(source_grads, val, NT, precision=lax.Precision.HIGHEST, preferred_element_type=f32)
    spread_ref[...] = jnp.broadcast_to(pair[None], spread_ref.shape)


def finish(parts_ref, sets_ref, pair_ref, set_ref):
    pair = jnp.sum(parts_ref[...], 0)
    pair_ref[...] = pair
    hot = jnp.where(sets_ref[...].astype(i32) == iota(sets_ref.shape, 0) + 1, 1.0, 0.0)
    total = lax.dot_general(hot, pair, NT, precision=lax.Precision.HIGHEST, preferred_element_type=f32)
    set_ref[...] = (total / jnp.sum(hot, 1, keepdims=True))[:SETS]


VMEM = pl.BlockSpec(memory_space=pltpu.VMEM)
SMEM = pl.BlockSpec(memory_space=pltpu.SMEM)
HBM = pl.BlockSpec(memory_space=pltpu.HBM)
PARAMS = pltpu.CompilerParams(vmem_limit_bytes=32 * 2**20)


def here(x):
    return pltpu.with_memory_space_constraint(x, pltpu.VMEM)


def far(x):
    return pltpu.with_memory_space_constraint(x, pltpu.HBM)


def call(kernel, out, specs, scratch=(), **kw):
    return pl.pallas_call(
        kernel,
        out_shape=out,
        in_specs=specs,
        out_specs=jax.tree.map(lambda _: VMEM, out),
        scratch_shapes=scratch,
        compiler_params=PARAMS,
        **kw,
    )


def exchange(blocks, axes):
    return lax.all_to_all(blocks, axes, 0, 0, tiled=True)


def local(act_in, grad_out, proj_in, proj_out, lengths, sources, val_feats, val_sets):
    rows = act_in.shape[0]
    place = jnp.stack([lax.axis_index(TENSOR), lax.axis_index("h"), lax.axis_index(DP)]).astype(i32)
    ints = jnp.concatenate([lengths, sources, val_sets[:, 0], place])
    part = call(
        project,
        pltpu.VMEM((rows, 2 * WIDTH), bf16),
        [HBM] * 4,
        [
            pltpu.VMEM(act_in.shape, bf16),
            pltpu.VMEM(grad_out.shape, bf16),
            pltpu.VMEM(proj_in.shape[::-1], bf16),
            pltpu.VMEM(proj_out.shape[::-1], bf16),
            pltpu.SemaphoreType.DMA((2 + 2 * PIECES,)),
        ],
    )(*(far(x) for x in (act_in, grad_out, proj_in.T, proj_out.T)))
    part = exchange(part.reshape(RANKS, MINE * SLOTS, 2 * WIDTH), TENSOR)
    block = call(
        gradients,
        pltpu.VMEM((HALVES * RANKS, 8, FEATS), bf16),
        [SMEM, VMEM, VMEM],
        [pltpu.VMEM((WIDTH, WIDTH), f32), pltpu.VMEM((8, FEATS), f32)],
    )(ints, here(part), val_feats)
    got = exchange(block, ("h",) + TENSOR)
    packed = call(pack, pltpu.VMEM((DESTS, 16, FEATS), bf16), [SMEM, VMEM])(ints, here(got))
    came = exchange(packed, ("y", "c"))
    source_grads, spread, sets = call(
        score,
        [
            jax.ShapeDtypeStruct((SRC_DEV, FEATS), f32),
            pltpu.VMEM((RANKS, SRC_DEV, NVAL), f32),
            pltpu.VMEM((8, NVAL), f32),
        ],
        [VMEM],
    )(here(came))
    parts = exchange(spread, TENSOR)
    pair_scores, set_scores = call(
        finish,
        [jax.ShapeDtypeStruct((SRC_DEV, NVAL), f32), jax.ShapeDtypeStruct((SETS, SRC_DEV), f32)],
        [VMEM, VMEM],
    )(here(parts), here(sets))
    return (source_grads, pair_scores, set_scores.T)


def solution(mesh):
    parts = Mesh(mesh.devices.reshape(SPLIT), NAMES)
    placed = (
        P(DP, TENSOR),
        P(DP, TENSOR),
        P(TENSOR, None),
        P(TENSOR, None),
        P(DP),
        P(DP),
        P(DP, TENSOR),
        P(DP, None),
    )
    return jax.shard_map(
        local,
        mesh=parts,
        in_specs=placed,
        out_specs=(P(DP, TENSOR), P(DP, None), P(DP, None)),
        check_vma=False,
    )
```

```python
import jax
import jax.numpy as jnp
from jax import lax
from jax.experimental import pallas as pl
from jax.experimental.pallas import tpu as pltpu
from jax.sharding import Mesh, PartitionSpec as P

SETS = 4
SRC_DEV = 8
SPLIT = (8, 2, 2, 4, 4)
NAMES = ("y", "h", "c", "z", "x")
DP = ("y", "h", "c")
TENSOR = ("z", "x")
HALVES, CORES, RANKS = 2, 2, 16
DESTS = 16
SEQS, SLOTS, WIDTH = 32, 32, 64
MINE = SEQS // RANKS
FEATS = WIDTH * WIDTH // RANKS
VALS = 4
NVAL = 128
CAP = 2
LOT = HALVES * CAP
NONE = 256.0
PIECES = 2
bf16, f32, i32 = jnp.bfloat16, jnp.float32, jnp.int32
NT = (((1,), (1,)), ((), ()))
TN = (((0,), (0,)), ((), ()))


def iota(shape, dim):
    return lax.broadcasted_iota(i32, shape, dim)


def tell(lengths, sources, sets, val, live_ref, base_ref, lay_ref):
    rank, half, dp = lax.axis_index(TENSOR), lax.axis_index("h"), lax.axis_index(DP)
    for q in range(MINE):
        cut = pl.ds(q * SLOTS, SLOTS)
        shape = (SLOTS, 2 * WIDTH)
        live_ref[cut, :] = jnp.where(iota(shape, 0) < lengths[rank * MINE + q], 1.0, 0.0)
    lane = iota((1, FEATS), 1)
    marks = jnp.zeros((1, FEATS), f32)
    for r in range(VALS):
        marks = jnp.where(lane == dp * VALS + r, (sets[0, r] + 1).astype(f32), marks)
    told = []
    for q in range(MINE):
        s = rank * MINE + q
        source = sources[s]
        owner = source // SRC_DEV
        order = jnp.int32(0)
        for other in range(SEQS):
            same = (sources[other] // SRC_DEV == owner) & (other < s)
            order = order + same.astype(i32)
        dest = owner // (HALVES * CORES) * CORES + owner % CORES
        told.append((owner // CORES % HALVES, dest * 16 + half * CAP + order, source % SRC_DEV + 1))
    shape = (RANKS, 8, FEATS)
    row, chunk = iota(shape, 1), iota(shape, 0)
    over = iota(shape, 2) % 16
    base_ref[0] = jnp.zeros((8, FEATS), f32)
    base_ref[0, 2 : 2 + VALS, :] = val[...].astype(f32)
    rows = jnp.broadcast_to(base_ref[0][None], shape)
    rows = jnp.where(chunk == rank, rows, jnp.where(row == 2, jnp.broadcast_to(marks[None], shape), 0.0))
    for h in range(HALVES):
        sent = rows
        for q in range(MINE):
            to, slot, tag = told[q]
            slot = jnp.where(to == h, slot, jnp.int32(NONE)).astype(f32)
            line = jnp.where(lane < 128, slot, tag.astype(f32))
            sent = jnp.where(row == 6 + q, jnp.broadcast_to(line[None], shape), sent)
        base_ref[pl.ds(h * RANKS, RANKS)] = sent
        is_val = (chunk == rank) & (over == LOT + h * VALS + row - 2)
        is_set = (chunk == (rank + 1) % RANKS) & (row == 2) & (over == LOT + HALVES * VALS)
        lay = (row >= 2) & (row < 2 + VALS) & (is_val | is_set)
        lay_ref[pl.ds(h * RANKS, RANKS)] = jnp.where(lay, 1.0, 0.0)


def project(*refs):
    sources, (part_ref, live_ref, base_ref, lay_ref), held, sems = refs[:8], refs[8:12], refs[12:20], refs[20]
    act, grad, pin, pout, lengths, owners, sets, val = held
    rows = act.shape[0] // PIECES
    moves = list(zip(sources[2:], held[2:]))
    for k in range(PIECES):
        cut = pl.ds(k * rows, rows)
        moves += [(sources[0].at[cut], act.at[cut]), (sources[1].at[cut], grad.at[cut])]
    copies = [pltpu.make_async_copy(*move, sems.at[i]) for i, move in enumerate(moves)]
    for copy in copies:
        copy.start()
    for copy in copies[2:6]:
        copy.wait()
    tell(lengths, owners, sets, val, live_ref, base_ref, lay_ref)
    copies[0].wait()
    copies[1].wait()
    for k in range(PIECES):
        cut = pl.ds(k * rows, rows)
        copies[6 + 2 * k].wait()
        copies[7 + 2 * k].wait()
        a = lax.dot_general(pin[...], act[cut, :], NT, preferred_element_type=f32)
        g = lax.dot_general(pout[...], grad[cut, :], NT, preferred_element_type=f32)
        part_ref[cut, :] = jnp.concatenate([a, g], 0).T.astype(bf16)


def gradients(part_ref, live_ref, base_ref, out_ref, square):
    whole = jnp.sum(part_ref[...].astype(f32), 0)
    whole = jnp.where(live_ref[...] > 0.0, whole, 0.0)
    flat = []
    for q in range(MINE):
        rows = whole[q * SLOTS : (q + 1) * SLOTS]
        square[q] = lax.dot_general(
            rows[:, WIDTH:], rows[:, :WIDTH], TN, precision=lax.Precision.HIGHEST, preferred_element_type=f32
        )
        step = WIDTH // RANKS
        lines = [square[q, pl.ds(r, RANKS, stride=step), :] for r in range(step)]
        flat.append(jnp.concatenate(lines, 1))
    shape = (RANKS, 8, FEATS)
    row = iota(shape, 1)
    for h in range(HALVES):
        cut = pl.ds(h * RANKS, RANKS)
        sent = base_ref[cut]
        for q in range(MINE):
            sent = jnp.where(row == q, jnp.broadcast_to(flat[q][:, None, :], shape), sent)
        out_ref[cut] = sent.astype(bf16)


def pack(got_ref, lay_ref, out_ref):
    x = got_ref[...].astype(f32)
    row, lane = iota(x.shape, 1), iota(x.shape, 2)
    turned = pltpu.roll(x, 2, 1)
    slot = jnp.concatenate([turned[:, :, :128]] * 2, 2).astype(i32)
    told = jnp.concatenate([x[:, :, :128]] * 2, 2).astype(i32)
    moves = ((row < 2) & (slot == lane)) | ((row >= 6) & (told + LOT + HALVES * VALS == lane))
    moves = jnp.where(moves, 1.0, lay_ref[...]).reshape(-1, FEATS).astype(bf16)
    x = jnp.where((row >= 6) & (lane < 128), 0.0, x).reshape(-1, FEATS).astype(bf16)
    packed = lax.dot_general(moves, x, TN, preferred_element_type=f32)
    out_ref[...] = packed.astype(bf16).reshape(out_ref.shape)


def score(came_ref, grads_ref, spread_ref, sets_ref):
    x = came_ref[...].astype(f32).reshape(-1, FEATS)
    rows = x.shape[0]
    half = x[:, :128]
    row = iota(half.shape, 0) % 16
    tags = pltpu.roll(x, rows - (LOT + HALVES * VALS), 0)[:, 128:].astype(i32)
    chooser = jnp.where((row < LOT) & (tags == iota(half.shape, 1) + 1), 1.0, 0.0).astype(bf16)
    x = x.astype(bf16)
    source_grads = lax.dot_general(chooser, x, TN, preferred_element_type=f32)[:SRC_DEV]
    grads_ref[...] = source_grads
    sets_ref[...] = jnp.broadcast_to(
        jnp.sum(jnp.where(row == LOT + HALVES * VALS, half, 0.0), 0, keepdims=True), sets_ref.shape
    )
    v, n = iota((NVAL, rows), 0), iota((NVAL, rows), 1)
    r, c, h, y = v % VALS, v // VALS % CORES, v // (VALS * CORES) % HALVES, v // (VALS * CORES * HALVES)
    pick = n == (y * CORES + c) * 16 + LOT + h * VALS + r
    val = jnp.dot(jnp.where(pick, 1.0, 0.0).astype(bf16), x, preferred_element_type=f32)
    pair = lax.dot_general(source_grads, val, NT, precision=lax.Precision.HIGHEST, preferred_element_type=f32)
    spread_ref[...] = jnp.broadcast_to(pair[None], spread_ref.shape)


def finish(parts_ref, sets_ref, grads_ref, pair_ref, set_ref, out_ref):
    out_ref[...] = grads_ref[...]
    pair = jnp.sum(parts_ref[...], 0)
    pair_ref[...] = pair
    hot = jnp.where(sets_ref[...].astype(i32) == iota(sets_ref.shape, 0) + 1, 1.0, 0.0)
    total = lax.dot_general(hot, pair, NT, precision=lax.Precision.HIGHEST, preferred_element_type=f32)
    set_ref[...] = (total / jnp.sum(hot, 1, keepdims=True))[:SETS]


VMEM = pl.BlockSpec(memory_space=pltpu.VMEM)
HBM = pl.BlockSpec(memory_space=pltpu.HBM)
PARAMS = pltpu.CompilerParams(vmem_limit_bytes=32 * 2**20)


def here(x):
    return pltpu.with_memory_space_constraint(x, pltpu.VMEM)


def far(x):
    return pltpu.with_memory_space_constraint(x, pltpu.HBM)


def call(kernel, out, specs, scratch=(), **kw):
    return pl.pallas_call(
        kernel,
        out_shape=out,
        in_specs=specs,
        out_specs=jax.tree.map(lambda _: VMEM, out),
        scratch_shapes=scratch,
        compiler_params=PARAMS,
        **kw,
    )


def exchange(blocks, axes):
    return lax.all_to_all(blocks, axes, 0, 0, tiled=True)


def local(act_in, grad_out, proj_in, proj_out, lengths, sources, val_feats, val_sets):
    rows = act_in.shape[0]
    chunks = (HALVES * RANKS, 8, FEATS)
    args = (act_in, grad_out, proj_in.T, proj_out.T, lengths, sources, val_sets.T, val_feats)
    homes = [pltpu.VMEM] * 4 + [pltpu.SMEM] * 3 + [pltpu.VMEM]
    part, live, base, lay = call(
        project,
        [
            pltpu.VMEM((rows, 2 * WIDTH), bf16),
            pltpu.VMEM((MINE * SLOTS, 2 * WIDTH), f32),
            pltpu.VMEM(chunks, f32),
            pltpu.VMEM(chunks, f32),
        ],
        [HBM] * 8,
        [home(x.shape, x.dtype) for home, x in zip(homes, args)] + [pltpu.SemaphoreType.DMA((6 + 2 * PIECES,))],
    )(*(far(x) for x in args))
    part = exchange(part.reshape(RANKS, MINE * SLOTS, 2 * WIDTH), TENSOR)
    block = call(gradients, pltpu.VMEM(chunks, bf16), [VMEM] * 3, [pltpu.VMEM((MINE, WIDTH, WIDTH), f32)])(
        here(part), here(live), here(base)
    )
    got = exchange(block, ("h",) + TENSOR)
    packed = call(pack, pltpu.VMEM((DESTS, 16, FEATS), bf16), [VMEM] * 2)(here(got), here(lay))
    came = exchange(packed, ("y", "c"))
    source_grads, spread, sets = call(
        score,
        [
            pltpu.VMEM((SRC_DEV, FEATS), f32),
            pltpu.VMEM((RANKS, SRC_DEV, NVAL), f32),
            pltpu.VMEM((8, NVAL), f32),
        ],
        [VMEM],
    )(here(came))
    parts = exchange(spread, TENSOR)
    pair_scores, set_scores, source_grads = call(
        finish,
        [
            jax.ShapeDtypeStruct((SRC_DEV, NVAL), f32),
            jax.ShapeDtypeStruct((SETS, SRC_DEV), f32),
            jax.ShapeDtypeStruct((SRC_DEV, FEATS), f32),
        ],
        [VMEM] * 3,
    )(here(parts), here(sets), here(source_grads))
    return (source_grads, pair_scores, set_scores.T)


def solution(mesh):
    parts = Mesh(mesh.devices.reshape(SPLIT), NAMES)
    placed = (
        P(DP, TENSOR),
        P(DP, TENSOR),
        P(TENSOR, None),
        P(TENSOR, None),
        P(DP),
        P(DP),
        P(DP, TENSOR),
        P(DP, None),
    )
    return jax.shard_map(
        local,
        mesh=parts,
        in_specs=placed,
        out_specs=(P(DP, TENSOR), P(DP, None), P(DP, None)),
        check_vma=False,
    )
```

```python
import jax
import jax.numpy as jnp
from jax import lax
from jax.experimental import pallas as pl
from jax.experimental.pallas import tpu as pltpu
from jax.sharding import Mesh, PartitionSpec as P

SETS = 4
SRC_DEV = 8
SPLIT = (8, 2, 2, 4, 4)
NAMES = ("y", "h", "c", "z", "x")
DP = ("y", "h", "c")
TENSOR = ("z", "x")
HALVES, CORES, RANKS = 2, 2, 16
DESTS = 16
SEQS, SLOTS, WIDTH = 32, 32, 64
MINE = SEQS // RANKS
FEATS = WIDTH * WIDTH // RANKS
VALS = 4
NVAL = 128
CAP = 2
LOT = HALVES * CAP
NONE = 256.0
CUTS = (0, 256, 512, 1024, 1536, 1792)
bf16, f32, i32 = jnp.bfloat16, jnp.float32, jnp.int32
NT = (((1,), (1,)), ((), ()))
TN = (((0,), (0,)), ((), ()))


def iota(shape, dim):
    return lax.broadcasted_iota(i32, shape, dim)


def tell(lengths, sources, sets, val, live_ref, base_ref, lay_ref):
    rank, half, dp = lax.axis_index(TENSOR), lax.axis_index("h"), lax.axis_index(DP)
    for q in range(MINE):
        slot = iota((WIDTH, 2 * WIDTH), 1) - q * SLOTS
        live_ref[q] = jnp.where((slot >= 0) & (slot < lengths[rank * MINE + q]), 1.0, 0.0)
    lane = iota((1, FEATS), 1)
    marks = jnp.zeros((1, FEATS), f32)
    for r in range(VALS):
        marks = jnp.where(lane == dp * VALS + r, (sets[0, r] + 1).astype(f32), marks)
    told = []
    for q in range(MINE):
        s = rank * MINE + q
        source = sources[s]
        owner = source // SRC_DEV
        order = jnp.int32(0)
        for other in range(SEQS):
            same = (sources[other] // SRC_DEV == owner) & (other < s)
            order = order + same.astype(i32)
        dest = owner // (HALVES * CORES) * CORES + owner % CORES
        told.append((owner // CORES % HALVES, dest * 16 + half * CAP + order, source % SRC_DEV + 1))
    shape = (RANKS, 8, FEATS)
    row, chunk = iota(shape, 1), iota(shape, 0)
    over = iota(shape, 2) % 16
    base_ref[0] = jnp.zeros((8, FEATS), f32)
    base_ref[0, 2 : 2 + VALS, :] = val[...].astype(f32)
    rows = jnp.broadcast_to(base_ref[0][None], shape)
    rows = jnp.where(chunk == rank, rows, jnp.where(row == 2, jnp.broadcast_to(marks[None], shape), 0.0))
    for h in range(HALVES):
        sent = rows
        for q in range(MINE):
            to, slot, tag = told[q]
            slot = jnp.where(to == h, slot, jnp.int32(NONE)).astype(f32)
            line = jnp.where(lane < 128, slot, tag.astype(f32))
            sent = jnp.where(row == 6 + q, jnp.broadcast_to(line[None], shape), sent)
        base_ref[pl.ds(h * RANKS, RANKS)] = sent
        is_val = (chunk == rank) & (over == LOT + h * VALS + row - 2)
        is_set = (chunk == (rank + 1) % RANKS) & (row == 2) & (over == LOT + HALVES * VALS)
        lay = (row >= 2) & (row < 2 + VALS) & (is_val | is_set)
        lay_ref[pl.ds(h * RANKS, RANKS)] = jnp.where(lay, 1.0, 0.0)


def project(*refs):
    sources, (part_ref, live_ref, base_ref, lay_ref), held, sems = refs[:8], refs[8:12], refs[12:20], refs[20]
    act, grad, pin, pout, lengths, owners, sets, val = held
    moves = [(sources[i], held[i]) for i in (4, 5, 6, 7, 3, 1, 2)]
    cuts = [pl.ds(lo, hi - lo) for lo, hi in zip(CUTS[:-1], CUTS[1:])]
    moves += [(sources[0].at[:, cut], act.at[:, cut]) for cut in cuts]
    copies = [pltpu.make_async_copy(*move, sems.at[i]) for i, move in enumerate(moves)]
    for copy in copies:
        copy.start()
    for copy in copies[:4]:
        copy.wait()
    tell(lengths, owners, sets, val, live_ref, base_ref, lay_ref)
    copies[4].wait()
    copies[5].wait()
    out = lax.dot_general(pout[...], grad[...], NT, preferred_element_type=f32)
    copies[6].wait()
    total = None
    for cut, copy in zip(cuts, copies[7:]):
        copy.wait()
        term = lax.dot_general(pin[:, cut], act[:, cut], NT, preferred_element_type=f32)
        total = term if total is None else total + term
    tokens = MINE * SLOTS
    for j in range(RANKS):
        cut = slice(j * tokens, (j + 1) * tokens)
        part_ref[j] = jnp.concatenate([total[:, cut], out[:, cut]], 1).astype(bf16)


def gradients(part_ref, live_ref, base_ref, out_ref, square):
    whole = jnp.sum(part_ref[...].astype(f32), 0)
    turned = pltpu.roll(whole, MINE * SLOTS, 1)
    flat = []
    for q in range(MINE):
        square[q] = lax.dot_general(
            jnp.where(live_ref[q] > 0.0, turned, 0.0),
            whole,
            NT,
            precision=lax.Precision.HIGHEST,
            preferred_element_type=f32,
        )
        step = WIDTH // RANKS
        lines = [square[q, pl.ds(r, RANKS, stride=step), :] for r in range(step)]
        flat.append(jnp.concatenate(lines, 1))
    shape = (RANKS, 8, FEATS)
    row = iota(shape, 1)
    for h in range(HALVES):
        cut = pl.ds(h * RANKS, RANKS)
        sent = base_ref[cut]
        for q in range(MINE):
            sent = jnp.where(row == q, jnp.broadcast_to(flat[q][:, None, :], shape), sent)
        out_ref[cut] = sent.astype(bf16)


def pack(got_ref, lay_ref, out_ref):
    x = got_ref[...].astype(f32)
    row, lane = iota(x.shape, 1), iota(x.shape, 2)
    turned = pltpu.roll(x, 2, 1)
    slot = jnp.concatenate([turned[:, :, :128]] * 2, 2).astype(i32)
    told = jnp.concatenate([x[:, :, :128]] * 2, 2).astype(i32)
    moves = ((row < 2) & (slot == lane)) | ((row >= 6) & (told + LOT + HALVES * VALS == lane))
    moves = jnp.where(moves, 1.0, lay_ref[...]).reshape(-1, FEATS).astype(bf16)
    x = jnp.where((row >= 6) & (lane < 128), 0.0, x).reshape(-1, FEATS).astype(bf16)
    packed = lax.dot_general(moves, x, TN, preferred_element_type=f32)
    out_ref[...] = packed.astype(bf16).reshape(out_ref.shape)


def score(came_ref, grads_ref, spread_ref, sets_ref):
    x = came_ref[...].astype(f32).reshape(-1, FEATS)
    rows = x.shape[0]
    half = x[:, :128]
    row = iota(half.shape, 0) % 16
    tags = pltpu.roll(x, rows - (LOT + HALVES * VALS), 0)[:, 128:].astype(i32)
    chooser = jnp.where((row < LOT) & (tags == iota(half.shape, 1) + 1), 1.0, 0.0).astype(bf16)
    x = x.astype(bf16)
    source_grads = lax.dot_general(chooser, x, TN, preferred_element_type=f32)[:SRC_DEV]
    grads_ref[...] = source_grads
    sets_ref[...] = jnp.broadcast_to(
        jnp.sum(jnp.where(row == LOT + HALVES * VALS, half, 0.0), 0, keepdims=True), sets_ref.shape
    )
    v, n = iota((NVAL, rows), 0), iota((NVAL, rows), 1)
    r, c, h, y = v % VALS, v // VALS % CORES, v // (VALS * CORES) % HALVES, v // (VALS * CORES * HALVES)
    pick = n == (y * CORES + c) * 16 + LOT + h * VALS + r
    val = jnp.dot(jnp.where(pick, 1.0, 0.0).astype(bf16), x, preferred_element_type=f32)
    pair = lax.dot_general(source_grads, val, NT, precision=lax.Precision.HIGHEST, preferred_element_type=f32)
    spread_ref[...] = jnp.broadcast_to(pair[None], spread_ref.shape)


def finish(parts_ref, sets_ref, grads_ref, pair_ref, set_ref, out_ref):
    out_ref[...] = grads_ref[...]
    pair = jnp.sum(parts_ref[...], 0)
    pair_ref[...] = pair
    hot = jnp.where(sets_ref[...].astype(i32) == iota(sets_ref.shape, 0) + 1, 1.0, 0.0)
    total = lax.dot_general(hot, pair, NT, precision=lax.Precision.HIGHEST, preferred_element_type=f32)
    set_ref[...] = (total / jnp.sum(hot, 1, keepdims=True))[:SETS]


VMEM = pl.BlockSpec(memory_space=pltpu.VMEM)
HBM = pl.BlockSpec(memory_space=pltpu.HBM)
PARAMS = pltpu.CompilerParams(vmem_limit_bytes=32 * 2**20)


def here(x):
    return pltpu.with_memory_space_constraint(x, pltpu.VMEM)


def far(x):
    return pltpu.with_memory_space_constraint(x, pltpu.HBM)


def call(kernel, out, specs, scratch=(), **kw):
    return pl.pallas_call(
        kernel,
        out_shape=out,
        in_specs=specs,
        out_specs=jax.tree.map(lambda _: VMEM, out),
        scratch_shapes=scratch,
        compiler_params=PARAMS,
        **kw,
    )


def exchange(blocks, axes):
    return lax.all_to_all(blocks, axes, 0, 0, tiled=True)


def local(act_in, grad_out, proj_in, proj_out, lengths, sources, val_feats, val_sets):
    chunks = (HALVES * RANKS, 8, FEATS)
    args = (act_in, grad_out, proj_in.T, proj_out.T, lengths, sources, val_sets.T, val_feats)
    homes = [pltpu.VMEM] * 4 + [pltpu.SMEM] * 3 + [pltpu.VMEM]
    part, live, base, lay = call(
        project,
        [
            pltpu.VMEM((RANKS, WIDTH, 2 * MINE * SLOTS), bf16),
            pltpu.VMEM((MINE, WIDTH, 2 * WIDTH), f32),
            pltpu.VMEM(chunks, f32),
            pltpu.VMEM(chunks, f32),
        ],
        [HBM] * 8,
        [home(x.shape, x.dtype) for home, x in zip(homes, args)] + [pltpu.SemaphoreType.DMA((6 + len(CUTS),))],
    )(*(far(x) for x in args))
    part = exchange(part, TENSOR)
    block = call(gradients, pltpu.VMEM(chunks, bf16), [VMEM] * 3, [pltpu.VMEM((MINE, WIDTH, WIDTH), f32)])(
        here(part), here(live), here(base)
    )
    got = exchange(block, ("h",) + TENSOR)
    packed = call(pack, pltpu.VMEM((DESTS, 16, FEATS), bf16), [VMEM] * 2)(here(got), here(lay))
    came = exchange(packed, ("y", "c"))
    source_grads, spread, sets = call(
        score,
        [
            pltpu.VMEM((SRC_DEV, FEATS), f32),
            pltpu.VMEM((RANKS, SRC_DEV, NVAL), f32),
            pltpu.VMEM((8, NVAL), f32),
        ],
        [VMEM],
    )(here(came))
    parts = exchange(spread, TENSOR)
    pair_scores, set_scores, source_grads = call(
        finish,
        [
            jax.ShapeDtypeStruct((SRC_DEV, NVAL), f32),
            jax.ShapeDtypeStruct((SETS, SRC_DEV), f32),
            jax.ShapeDtypeStruct((SRC_DEV, FEATS), f32),
        ],
        [VMEM] * 3,
    )(here(parts), here(sets), here(source_grads))
    return (source_grads, pair_scores, set_scores.T)


def solution(mesh):
    parts = Mesh(mesh.devices.reshape(SPLIT), NAMES)
    placed = (
        P(DP, TENSOR),
        P(DP, TENSOR),
        P(TENSOR, None),
        P(TENSOR, None),
        P(DP),
        P(DP),
        P(DP, TENSOR),
        P(DP, None),
    )
    return jax.shard_map(
        local,
        mesh=parts,
        in_specs=placed,
        out_specs=(P(DP, TENSOR), P(DP, None), P(DP, None)),
        check_vma=False,
    )
```

```python
import jax
import jax.numpy as jnp
from jax import lax
from jax.experimental import pallas as pl
from jax.experimental.pallas import tpu as pltpu
from jax.sharding import Mesh, PartitionSpec as P

SETS = 4
SRC_DEV = 8
SPLIT = (8, 2, 2, 4, 4)
NAMES = ("y", "h", "c", "z", "x")
DP = ("y", "h", "c")
TENSOR = ("z", "x")
HALVES, CORES, RANKS = 2, 2, 16
DESTS = 16
SEQS, SLOTS, WIDTH = 32, 32, 64
MINE = SEQS // RANKS
FEATS = WIDTH * WIDTH // RANKS
VALS = 4
NVAL = 128
CAP = 2
LOT = HALVES * CAP
LINE = 3 * FEATS + 128
NONE = 256.0
MARK = 136
CUTS = (0, 256, 512, 1024, 1536, 1792)
bf16, f32, i32 = jnp.bfloat16, jnp.float32, jnp.int32
NT = (((1,), (1,)), ((), ()))
TN = (((0,), (0,)), ((), ()))


def iota(shape, dim):
    return lax.broadcasted_iota(i32, shape, dim)


def tell(lengths, sources, sets, val, live_ref, base_ref, lay_ref, mark_ref):
    rank, half = lax.axis_index(TENSOR), lax.axis_index("h")
    for q in range(MINE):
        slot = iota((WIDTH, 2 * WIDTH), 1) - q * SLOTS
        live_ref[q] = jnp.where((slot >= 0) & (slot < lengths[rank * MINE + q]), 1.0, 0.0)
    lane = iota((1, FEATS), 1)
    marks = jnp.zeros((1, FEATS), f32)
    for r in range(VALS):
        marks = jnp.where(lane == MARK + half * VALS + r, (sets[0, r] + 1).astype(f32), marks)
    told = []
    for q in range(MINE):
        s = rank * MINE + q
        source = sources[s]
        owner = source // SRC_DEV
        order = jnp.int32(0)
        for other in range(SEQS):
            same = (sources[other] // SRC_DEV == owner) & (other < s)
            order = order + same.astype(i32)
        dest = owner // (HALVES * CORES) * CORES + owner % CORES
        told.append((owner // CORES % HALVES, dest * 8 + half * CAP + order, source % SRC_DEV + 1))
    shape = (RANKS, 8, FEATS)
    row, chunk = iota(shape, 1), iota(shape, 0)
    over, odd = iota(shape, 2) % 8, iota(shape, 2) // 128
    base_ref[0] = jnp.zeros((8, FEATS), f32)
    base_ref[0, 2 : 2 + VALS, :] = val[...].astype(f32)
    rows = jnp.broadcast_to(base_ref[0][None], shape)
    rows = jnp.where(chunk == rank, rows, jnp.where(row == 2, jnp.broadcast_to(marks[None], shape), 0.0))
    for h in range(HALVES):
        sent = rows
        for q in range(MINE):
            to, slot, tag = told[q]
            slot = jnp.where(to == h, slot, jnp.int32(NONE)).astype(f32)
            line = jnp.where(lane < 128, slot, jnp.where(lane < MARK, tag.astype(f32), 0.0))
            sent = jnp.where(row == 6 + q, jnp.broadcast_to(line[None], shape), sent)
        base_ref[pl.ds(h * RANKS, RANKS)] = sent
        which = h * VALS + row - 2
        lay = (chunk == rank) & (row >= 2) & (row < 2 + VALS) & (which % 2 == odd) & (which // 2 == over)
        lay_ref[pl.ds(h * RANKS, RANKS)] = jnp.where(lay, 1.0, 0.0)
        lay = (chunk == (rank + 1) % RANKS) & (row == 2) & (over == 0)
        mark_ref[pl.ds(h * RANKS, RANKS)] = jnp.where(lay, 1.0, 0.0)[:, :, :128]


def project(*refs):
    sources, (part_ref, *told), held, sems = refs[:8], refs[8:13], refs[13:21], refs[21]
    act, grad, pin, pout, lengths, owners, sets, val = held
    moves = [(sources[i], held[i]) for i in (4, 5, 6, 7, 3, 1, 2)]
    cuts = [pl.ds(lo, hi - lo) for lo, hi in zip(CUTS[:-1], CUTS[1:])]
    moves += [(sources[0].at[:, cut], act.at[:, cut]) for cut in cuts]
    copies = [pltpu.make_async_copy(*move, sems.at[i]) for i, move in enumerate(moves)]
    for copy in copies:
        copy.start()
    for copy in copies[:4]:
        copy.wait()
    tell(lengths, owners, sets, val, *told)
    copies[4].wait()
    copies[5].wait()
    out = lax.dot_general(pout[...], grad[...], NT, preferred_element_type=f32)
    copies[6].wait()
    total = None
    for cut, copy in zip(cuts, copies[7:]):
        copy.wait()
        term = lax.dot_general(pin[:, cut], act[:, cut], NT, preferred_element_type=f32)
        total = term if total is None else total + term
    tokens = MINE * SLOTS
    for j in range(RANKS):
        cut = slice(j * tokens, (j + 1) * tokens)
        part_ref[j] = jnp.concatenate([total[:, cut], out[:, cut]], 1).astype(bf16)


def gradients(part_ref, live_ref, base_ref, out_ref, square):
    whole = jnp.sum(part_ref[...].astype(f32), 0)
    turned = pltpu.roll(whole, MINE * SLOTS, 1)
    flat = []
    for q in range(MINE):
        square[q] = lax.dot_general(
            jnp.where(live_ref[q] > 0.0, turned, 0.0),
            whole,
            NT,
            precision=lax.Precision.HIGHEST,
            preferred_element_type=f32,
        )
        step = WIDTH // RANKS
        lines = [square[q, pl.ds(r, RANKS, stride=step), :] for r in range(step)]
        flat.append(jnp.concatenate(lines, 1))
    shape = (RANKS, 8, FEATS)
    row = iota(shape, 1)
    for h in range(HALVES):
        cut = pl.ds(h * RANKS, RANKS)
        sent = base_ref[cut]
        for q in range(MINE):
            sent = jnp.where(row == q, jnp.broadcast_to(flat[q][:, None, :], shape), sent)
        out_ref[cut] = sent.astype(bf16)


def pack(got_ref, lay_ref, mark_ref, out_ref):
    x = got_ref[...].astype(f32)
    told = x[:, :, :128].astype(i32)
    slot = pltpu.roll(x[:, :, :128], 2, 1).astype(i32)
    row, lane = iota(told.shape, 1), iota(told.shape, 2)
    grads = jnp.where((row < 2) & (slot == lane), 1.0, 0.0)
    marks = jnp.where((row >= 6) & (told == lane), 1.0, mark_ref[...])
    moves = jnp.concatenate([grads, lay_ref[...], marks], 2).reshape(-1, 512).astype(bf16)
    x = x.reshape(-1, FEATS).astype(bf16)
    packed = lax.dot_general(moves[:, :384], x, TN, preferred_element_type=f32)
    small = lax.dot_general(moves[:, 384:], x[:, 128:], TN, preferred_element_type=f32)
    pieces = [packed[k * 128 : (k + 1) * 128].reshape(DESTS, 8, FEATS) for k in range(3)]
    pieces.append(small.reshape(DESTS, 8, 128))
    out_ref[...] = jnp.concatenate(pieces, 2)[:, :LOT].astype(bf16)


def score(came_ref, grads_ref, spread_ref, sets_ref):
    x = came_ref[...].astype(f32)
    x = jnp.concatenate([x, jnp.zeros(x.shape, f32)], 1).reshape(DESTS * 8, LINE)
    small = x[:, 3 * FEATS :]
    n, lane = iota(small.shape, 0), iota(small.shape, 1)
    chooser = jnp.where(small.astype(i32) == lane + 1, 1.0, 0.0).astype(bf16)
    x = x.astype(bf16)
    source_grads = lax.dot_general(chooser, x[:, :FEATS], TN, preferred_element_type=f32)[:SRC_DEV]
    grads_ref[...] = source_grads

    def parts(v):
        return v % VALS, v // VALS % CORES, v // (VALS * CORES) % HALVES, v // (VALS * CORES * HALVES)

    r, c, h, y = parts(lane)
    spread = jnp.where(n == MARK - 128 + h * VALS + r, 1.0, 0.0).astype(bf16)
    marks = jnp.dot(small.astype(bf16), spread, preferred_element_type=f32)
    marks = jnp.sum(jnp.where(n == (y * CORES + c) * 8, marks, 0.0), 0, keepdims=True)
    sets_ref[...] = jnp.broadcast_to(marks, sets_ref.shape)
    shape = (NVAL, 2 * DESTS * 8)
    r, c, h, y = parts(iota(shape, 0))
    pick = iota(shape, 1) == r % 2 * (DESTS * 8) + (y * CORES + c) * 8 + (h * VALS + r) // 2
    val = jnp.concatenate([x[:, FEATS : 2 * FEATS], x[:, 2 * FEATS : 3 * FEATS]], 0)
    val = jnp.dot(jnp.where(pick, 1.0, 0.0).astype(bf16), val, preferred_element_type=f32)
    pair = lax.dot_general(source_grads, val, NT, precision=lax.Precision.HIGHEST, preferred_element_type=f32)
    spread_ref[...] = jnp.broadcast_to(pair[None], spread_ref.shape)


def finish(parts_ref, sets_ref, grads_ref, pair_ref, set_ref, out_ref):
    out_ref[...] = grads_ref[...]
    pair = jnp.sum(parts_ref[...], 0)
    pair_ref[...] = pair
    hot = jnp.where(sets_ref[...].astype(i32) == iota(sets_ref.shape, 0) + 1, 1.0, 0.0)
    total = lax.dot_general(hot, pair, NT, precision=lax.Precision.HIGHEST, preferred_element_type=f32)
    set_ref[...] = (total / jnp.sum(hot, 1, keepdims=True))[:SETS]


VMEM = pl.BlockSpec(memory_space=pltpu.VMEM)
HBM = pl.BlockSpec(memory_space=pltpu.HBM)
PARAMS = pltpu.CompilerParams(vmem_limit_bytes=32 * 2**20)


def here(x):
    return pltpu.with_memory_space_constraint(x, pltpu.VMEM)


def far(x):
    return pltpu.with_memory_space_constraint(x, pltpu.HBM)


def call(kernel, out, specs, scratch=(), **kw):
    return pl.pallas_call(
        kernel,
        out_shape=out,
        in_specs=specs,
        out_specs=jax.tree.map(lambda _: VMEM, out),
        scratch_shapes=scratch,
        compiler_params=PARAMS,
        **kw,
    )


def exchange(blocks, axes):
    return lax.all_to_all(blocks, axes, 0, 0, tiled=True)


def local(act_in, grad_out, proj_in, proj_out, lengths, sources, val_feats, val_sets):
    chunks = (HALVES * RANKS, 8, FEATS)
    args = (act_in, grad_out, proj_in.T, proj_out.T, lengths, sources, val_sets.T, val_feats)
    homes = [pltpu.VMEM] * 4 + [pltpu.SMEM] * 3 + [pltpu.VMEM]
    part, live, base, lay, mark = call(
        project,
        [
            pltpu.VMEM((RANKS, WIDTH, 2 * MINE * SLOTS), bf16),
            pltpu.VMEM((MINE, WIDTH, 2 * WIDTH), f32),
            pltpu.VMEM(chunks, f32),
            pltpu.VMEM(chunks, f32),
            pltpu.VMEM(chunks[:2] + (128,), f32),
        ],
        [HBM] * 8,
        [home(x.shape, x.dtype) for home, x in zip(homes, args)] + [pltpu.SemaphoreType.DMA((6 + len(CUTS),))],
    )(*(far(x) for x in args))
    part = exchange(part, TENSOR)
    block = call(gradients, pltpu.VMEM(chunks, bf16), [VMEM] * 3, [pltpu.VMEM((MINE, WIDTH, WIDTH), f32)])(
        here(part), here(live), here(base)
    )
    got = exchange(block, ("h",) + TENSOR)
    packed = call(pack, pltpu.VMEM((DESTS, LOT, LINE), bf16), [VMEM] * 3)(here(got), here(lay), here(mark))
    came = exchange(packed, ("y", "c"))
    source_grads, spread, sets = call(
        score,
        [
            pltpu.VMEM((SRC_DEV, FEATS), f32),
            pltpu.VMEM((RANKS, SRC_DEV, NVAL), f32),
            pltpu.VMEM((8, NVAL), f32),
        ],
        [VMEM],
    )(here(came))
    parts = exchange(spread, TENSOR)
    pair_scores, set_scores, source_grads = call(
        finish,
        [
            jax.ShapeDtypeStruct((SRC_DEV, NVAL), f32),
            jax.ShapeDtypeStruct((SETS, SRC_DEV), f32),
            jax.ShapeDtypeStruct((SRC_DEV, FEATS), f32),
        ],
        [VMEM] * 3,
    )(here(parts), here(sets), here(source_grads))
    return (source_grads, pair_scores, set_scores.T)


def solution(mesh):
    parts = Mesh(mesh.devices.reshape(SPLIT), NAMES)
    placed = (
        P(DP, TENSOR),
        P(DP, TENSOR),
        P(TENSOR, None),
        P(TENSOR, None),
        P(DP),
        P(DP),
        P(DP, TENSOR),
        P(DP, None),
    )
    return jax.shard_map(
        local,
        mesh=parts,
        in_specs=placed,
        out_specs=(P(DP, TENSOR), P(DP, None), P(DP, None)),
        check_vma=False,
    )
```

```python
import jax
import jax.numpy as jnp
from jax import lax
from jax.experimental import pallas as pl
from jax.experimental.pallas import tpu as pltpu
from jax.sharding import Mesh, PartitionSpec as P

SETS = 4
SRC_DEV = 8
SPLIT = (8, 2, 2, 4, 4)
NAMES = ("y", "h", "c", "z", "x")
DP = ("y", "h", "c")
TENSOR = ("z", "x")
HALVES, CORES, RANKS = 2, 2, 16
DESTS = 16
SEQS, SLOTS, WIDTH = 32, 32, 64
MINE = SEQS // RANKS
FEATS = WIDTH * WIDTH // RANKS
VALS = 4
NVAL = 128
CAP = 2
LOT = HALVES * CAP
LINE = 3 * FEATS + 128
REST = LINE - FEATS
MARK = 8
SLOT = 2 * FEATS + 64
NONE = 256.0
CUTS = (0, 256, 512, 1024, 1536, 1792)
bf16, f32, i32 = jnp.bfloat16, jnp.float32, jnp.int32
NT = (((1,), (1,)), ((), ()))
TN = (((0,), (0,)), ((), ()))


def iota(shape, dim):
    return lax.broadcasted_iota(i32, shape, dim)


def tell(lengths, sources, sets, val, live_ref, base_ref, lay_ref, mark_ref):
    rank, half = lax.axis_index(TENSOR), lax.axis_index("h")
    for q in range(MINE):
        slot = iota((WIDTH, 2 * WIDTH), 1) - q * SLOTS
        live_ref[q] = jnp.where((slot >= 0) & (slot < lengths[rank * MINE + q]), 1.0, 0.0)
    lane = iota((1, REST), 1)
    marks = jnp.zeros((1, REST), f32)
    for r in range(VALS):
        marks = jnp.where(lane == MARK + half * VALS + r, (sets[0, r] + 1).astype(f32), marks)
    told = []
    for q in range(MINE):
        s = rank * MINE + q
        source = sources[s]
        owner = source // SRC_DEV
        order = jnp.int32(0)
        for other in range(SEQS):
            same = (sources[other] // SRC_DEV == owner) & (other < s)
            order = order + same.astype(i32)
        dest = owner // (HALVES * CORES) * CORES + owner % CORES
        told.append((owner // CORES % HALVES, dest * 8 + half * CAP + order, source % SRC_DEV + 1))
    shape = (RANKS, 8, REST)
    row, chunk = iota(shape, 1), iota(shape, 0)
    base_ref[0] = jnp.zeros((8, REST), f32)
    rows = val[...].astype(f32)
    for r in range(VALS):
        base_ref[0, r // 2 : r // 2 + 1, r % 2 * FEATS : (r % 2 + 1) * FEATS] = rows[r : r + 1]
    rows = jnp.broadcast_to(base_ref[0][None], shape)
    rows = jnp.where(chunk == rank, rows, jnp.where(row == 0, jnp.broadcast_to(marks[None], shape), 0.0))
    small = (RANKS, 8, 128)
    line, over, owner = iota(small, 1), iota(small, 2) % 8, iota(small, 0)
    for h in range(HALVES):
        cut = pl.ds(h * RANKS, RANKS)
        sent = rows
        for q in range(MINE):
            to, slot, tag = told[q]
            slot = jnp.where(to == h, slot, jnp.int32(NONE)).astype(f32)
            word = jnp.where(lane >= SLOT, slot, jnp.where(lane < 2 * FEATS + MARK, tag.astype(f32), 0.0))
            sent = jnp.where((row == q) & (iota(shape, 2) >= 2 * FEATS), jnp.broadcast_to(word[None], shape), sent)
        base_ref[cut] = sent
        lay = (owner == rank) & (line < MINE) & (over == h * MINE + line)
        lay_ref[cut] = jnp.where(lay, 1.0, 0.0)
        lay = (owner == (rank + 1) % RANKS) & (line == 0) & (over == 0)
        mark_ref[cut] = jnp.where(lay, 1.0, 0.0)


def project(*refs):
    sources, (part_ref, *told), held, sems = refs[:8], refs[8:13], refs[13:21], refs[21]
    act, grad, pin, pout, lengths, owners, sets, val = held
    moves = [(sources[i], held[i]) for i in (4, 5, 6, 7, 3, 1, 2)]
    cuts = [pl.ds(lo, hi - lo) for lo, hi in zip(CUTS[:-1], CUTS[1:])]
    moves += [(sources[0].at[:, cut], act.at[:, cut]) for cut in cuts]
    copies = [pltpu.make_async_copy(*move, sems.at[i]) for i, move in enumerate(moves)]
    for copy in copies:
        copy.start()
    for copy in copies[:4]:
        copy.wait()
    tell(lengths, owners, sets, val, *told)
    copies[4].wait()
    copies[5].wait()
    out = lax.dot_general(pout[...], grad[...], NT, preferred_element_type=f32)
    copies[6].wait()
    total = None
    for cut, copy in zip(cuts, copies[7:]):
        copy.wait()
        term = lax.dot_general(pin[:, cut], act[:, cut], NT, preferred_element_type=f32)
        total = term if total is None else total + term
    tokens = MINE * SLOTS
    for j in range(RANKS):
        cut = slice(j * tokens, (j + 1) * tokens)
        part_ref[j] = jnp.concatenate([total[:, cut], out[:, cut]], 1).astype(bf16)


def gradients(part_ref, live_ref, base_ref, out_ref, square):
    whole = jnp.sum(part_ref[...].astype(f32), 0)
    turned = pltpu.roll(whole, MINE * SLOTS, 1)
    flat = []
    for q in range(MINE):
        square[q] = lax.dot_general(
            jnp.where(live_ref[q] > 0.0, turned, 0.0),
            whole,
            NT,
            precision=lax.Precision.HIGHEST,
            preferred_element_type=f32,
        )
        step = WIDTH // RANKS
        lines = [square[q, pl.ds(r, RANKS, stride=step), :] for r in range(step)]
        flat.append(jnp.concatenate(lines, 1))
    shape = (RANKS, 8, FEATS)
    flat = [jnp.broadcast_to(line[:, None, :], shape) for line in flat]
    flat = jnp.where(iota(shape, 1) == 0, flat[0], flat[1])
    for h in range(HALVES):
        cut = pl.ds(h * RANKS, RANKS)
        out_ref[cut] = jnp.concatenate([flat, base_ref[cut]], 2)[:, :MINE].astype(bf16)


def pack(got_ref, lay_ref, mark_ref, out_ref):
    x = got_ref[...].astype(f32)
    x = jnp.concatenate([x, jnp.zeros((x.shape[0], 8 - MINE, LINE), f32)], 1)
    shape = x.shape[:2] + (128,)
    slot = jnp.broadcast_to(x[:, :, FEATS + SLOT : FEATS + SLOT + 1], shape).astype(i32)
    moves = jnp.where((iota(shape, 1) < MINE) & (slot == iota(shape, 2)), 1.0, 0.0)
    moves, lay, mark = (m.reshape(-1, 128).astype(bf16) for m in (moves, lay_ref[...], mark_ref[...]))
    x = x.reshape(-1, LINE).astype(bf16)
    own = jnp.concatenate([x[:, :FEATS], x[:, 3 * FEATS :]], 1)
    own = lax.dot_general(moves, own, TN, preferred_element_type=f32)
    val = lax.dot_general(lay, x[:, FEATS : 3 * FEATS], TN, preferred_element_type=f32)
    marks = lax.dot_general(mark, x[:, FEATS : FEATS + 128], TN, preferred_element_type=f32)
    out = jnp.concatenate([own[:, :FEATS], val, own[:, FEATS:] + marks], 1)
    out_ref[...] = out.reshape(DESTS, 8, LINE)[:, :LOT].astype(bf16)


def score(came_ref, grads_ref, spread_ref, sets_ref):
    x = came_ref[...].astype(f32)
    x = jnp.concatenate([x, jnp.zeros(x.shape, f32)], 1).reshape(DESTS * 8, LINE)
    small = x[:, 3 * FEATS :]
    n, lane = iota(small.shape, 0), iota(small.shape, 1)
    chooser = jnp.where(small.astype(i32) == lane + 1, 1.0, 0.0).astype(bf16)
    x = x.astype(bf16)
    source_grads = lax.dot_general(chooser, x[:, :FEATS], TN, preferred_element_type=f32)[:SRC_DEV]
    grads_ref[...] = source_grads

    def parts(v):
        return v % VALS, v // VALS % CORES, v // (VALS * CORES) % HALVES, v // (VALS * CORES * HALVES)

    r, c, h, y = parts(lane)
    spread = jnp.where(n == MARK + h * VALS + r, 1.0, 0.0).astype(bf16)
    marks = jnp.dot(small.astype(bf16), spread, preferred_element_type=f32)
    marks = jnp.sum(jnp.where(n == (y * CORES + c) * 8, marks, 0.0), 0, keepdims=True)
    sets_ref[...] = jnp.broadcast_to(marks, sets_ref.shape)
    shape = (NVAL, 2 * DESTS * 8)
    r, c, h, y = parts(iota(shape, 0))
    pick = iota(shape, 1) == r % 2 * (DESTS * 8) + (y * CORES + c) * 8 + (h * VALS + r) // 2
    val = jnp.concatenate([x[:, FEATS : 2 * FEATS], x[:, 2 * FEATS : 3 * FEATS]], 0)
    val = jnp.dot(jnp.where(pick, 1.0, 0.0).astype(bf16), val, preferred_element_type=f32)
    pair = lax.dot_general(source_grads, val, NT, precision=lax.Precision.HIGHEST, preferred_element_type=f32)
    spread_ref[...] = jnp.broadcast_to(pair[None], spread_ref.shape)


def finish(parts_ref, sets_ref, grads_ref, pair_ref, set_ref, out_ref):
    out_ref[...] = grads_ref[...]
    pair = jnp.sum(parts_ref[...], 0)
    pair_ref[...] = pair
    hot = jnp.where(sets_ref[...].astype(i32) == iota(sets_ref.shape, 0) + 1, 1.0, 0.0)
    total = lax.dot_general(hot, pair, NT, precision=lax.Precision.HIGHEST, preferred_element_type=f32)
    set_ref[...] = (total / jnp.sum(hot, 1, keepdims=True))[:SETS]


VMEM = pl.BlockSpec(memory_space=pltpu.VMEM)
HBM = pl.BlockSpec(memory_space=pltpu.HBM)
PARAMS = pltpu.CompilerParams(vmem_limit_bytes=32 * 2**20)


def here(x):
    return pltpu.with_memory_space_constraint(x, pltpu.VMEM)


def far(x):
    return pltpu.with_memory_space_constraint(x, pltpu.HBM)


def call(kernel, out, specs, scratch=(), **kw):
    return pl.pallas_call(
        kernel,
        out_shape=out,
        in_specs=specs,
        out_specs=jax.tree.map(lambda _: VMEM, out),
        scratch_shapes=scratch,
        compiler_params=PARAMS,
        **kw,
    )


def exchange(blocks, axes):
    return lax.all_to_all(blocks, axes, 0, 0, tiled=True)


def local(act_in, grad_out, proj_in, proj_out, lengths, sources, val_feats, val_sets):
    chunks = HALVES * RANKS
    args = (act_in, grad_out, proj_in.T, proj_out.T, lengths, sources, val_sets.T, val_feats)
    homes = [pltpu.VMEM] * 4 + [pltpu.SMEM] * 3 + [pltpu.VMEM]
    part, live, base, lay, mark = call(
        project,
        [
            pltpu.VMEM((RANKS, WIDTH, 2 * MINE * SLOTS), bf16),
            pltpu.VMEM((MINE, WIDTH, 2 * WIDTH), f32),
            pltpu.VMEM((chunks, 8, REST), f32),
            pltpu.VMEM((chunks, 8, 128), f32),
            pltpu.VMEM((chunks, 8, 128), f32),
        ],
        [HBM] * 8,
        [home(x.shape, x.dtype) for home, x in zip(homes, args)] + [pltpu.SemaphoreType.DMA((6 + len(CUTS),))],
    )(*(far(x) for x in args))
    part = exchange(part, TENSOR)
    block = call(gradients, pltpu.VMEM((chunks, MINE, LINE), bf16), [VMEM] * 3, [pltpu.VMEM((MINE, WIDTH, WIDTH), f32)])(
        here(part), here(live), here(base)
    )
    got = exchange(block, ("h",) + TENSOR)
    packed = call(pack, pltpu.VMEM((DESTS, LOT, LINE), bf16), [VMEM] * 3)(here(got), here(lay), here(mark))
    came = exchange(packed, ("y", "c"))
    source_grads, spread, sets = call(
        score,
        [
            pltpu.VMEM((SRC_DEV, FEATS), f32),
            pltpu.VMEM((RANKS, SRC_DEV, NVAL), f32),
            pltpu.VMEM((8, NVAL), f32),
        ],
        [VMEM],
    )(here(came))
    parts = exchange(spread, TENSOR)
    pair_scores, set_scores, source_grads = call(
        finish,
        [
            jax.ShapeDtypeStruct((SRC_DEV, NVAL), f32),
            jax.ShapeDtypeStruct((SETS, SRC_DEV), f32),
            jax.ShapeDtypeStruct((SRC_DEV, FEATS), f32),
        ],
        [VMEM] * 3,
    )(here(parts), here(sets), here(source_grads))
    return (source_grads, pair_scores, set_scores.T)


def solution(mesh):
    parts = Mesh(mesh.devices.reshape(SPLIT), NAMES)
    placed = (
        P(DP, TENSOR),
        P(DP, TENSOR),
        P(TENSOR, None),
        P(TENSOR, None),
        P(DP),
        P(DP),
        P(DP, TENSOR),
        P(DP, None),
    )
    return jax.shard_map(
        local,
        mesh=parts,
        in_specs=placed,
        out_specs=(P(DP, TENSOR), P(DP, None), P(DP, None)),
        check_vma=False,
    )
```

```python
import jax
import jax.numpy as jnp
from jax import lax
from jax.experimental import pallas as pl
from jax.experimental.pallas import tpu as pltpu
from jax.sharding import Mesh, PartitionSpec as P

SETS = 4
SRC_DEV = 8
SPLIT = (8, 2, 2, 4, 4)
NAMES = ("y", "h", "c", "z", "x")
DP = ("y", "h", "c")
TENSOR = ("z", "x")
HALVES, CORES, RANKS = 2, 2, 16
DESTS = 16
SEQS, SLOTS, WIDTH = 32, 32, 64
MINE = SEQS // RANKS
FEATS = WIDTH * WIDTH // RANKS
VALS = 4
NVAL = 128
CAP = 2
LOT = HALVES * CAP
LINE = 3 * FEATS + 128
REST = LINE - FEATS
MARK = 8
SLOT = 2 * FEATS + 64
NONE = 256.0
CUTS = (0, 256, 512, 1024, 1536, 1792)
bf16, f32, i32 = jnp.bfloat16, jnp.float32, jnp.int32
NT = (((1,), (1,)), ((), ()))
TN = (((0,), (0,)), ((), ()))


def iota(shape, dim):
    return lax.broadcasted_iota(i32, shape, dim)


def parts(v):
    return v % VALS, v // VALS % CORES, v // (VALS * CORES) % HALVES, v // (VALS * CORES * HALVES)


def fix(fixed_ref):
    shape = (NVAL, 2 * DESTS * 8)
    r, c, h, y = parts(iota(shape, 0))
    pick = iota(shape, 1) == r % 2 * (DESTS * 8) + (y * CORES + c) * 8 + (h * VALS + r) // 2
    fixed_ref[:, :256] = jnp.where(pick, 1.0, 0.0).astype(bf16)
    n, v = iota((128, NVAL), 0), iota((128, NVAL), 1)
    r, c, h, y = parts(v)
    fixed_ref[:, 256:384] = jnp.where(n == MARK + h * VALS + r, 1.0, 0.0).astype(bf16)
    fixed_ref[:, 384:] = jnp.where(n == (y * CORES + c) * 8, 1.0, 0.0).astype(bf16)


def tell(lengths, sources, sets, val, live_ref, base_ref, lay_ref, mark_ref):
    rank, half = lax.axis_index(TENSOR), lax.axis_index("h")
    for q in range(MINE):
        slot = iota((WIDTH, 2 * WIDTH), 1) - q * SLOTS
        live_ref[q * WIDTH : (q + 1) * WIDTH, :] = jnp.where((slot >= 0) & (slot < lengths[rank * MINE + q]), 1.0, 0.0)
    lane = iota((1, REST), 1)
    marks = jnp.zeros((1, REST), f32)
    for r in range(VALS):
        marks = jnp.where(lane == MARK + half * VALS + r, (sets[0, r] + 1).astype(f32), marks)
    told = []
    for q in range(MINE):
        s = rank * MINE + q
        source = sources[s]
        owner = source // SRC_DEV
        order = jnp.int32(0)
        for other in range(SEQS):
            same = (sources[other] // SRC_DEV == owner) & (other < s)
            order = order + same.astype(i32)
        dest = owner // (HALVES * CORES) * CORES + owner % CORES
        told.append((owner // CORES % HALVES, dest * 8 + half * CAP + order, source % SRC_DEV + 1))
    shape = (RANKS, 8, REST)
    row, chunk = iota(shape, 1), iota(shape, 0)
    base_ref[0] = jnp.zeros((8, REST), f32)
    rows = val[...].astype(f32)
    for r in range(VALS):
        base_ref[0, r // 2 : r // 2 + 1, r % 2 * FEATS : (r % 2 + 1) * FEATS] = rows[r : r + 1]
    rows = jnp.broadcast_to(base_ref[0][None], shape)
    rows = jnp.where(chunk == rank, rows, jnp.where(row == 0, jnp.broadcast_to(marks[None], shape), 0.0))
    small = (RANKS, 8, 128)
    line, over, owner = iota(small, 1), iota(small, 2) % 8, iota(small, 0)
    for h in range(HALVES):
        cut = pl.ds(h * RANKS, RANKS)
        sent = rows
        for q in range(MINE):
            to, slot, tag = told[q]
            slot = jnp.where(to == h, slot, jnp.int32(NONE)).astype(f32)
            word = jnp.where(lane >= SLOT, slot, jnp.where(lane < 2 * FEATS + MARK, tag.astype(f32), 0.0))
            sent = jnp.where((row == q) & (iota(shape, 2) >= 2 * FEATS), jnp.broadcast_to(word[None], shape), sent)
        base_ref[cut] = sent
        lay = (owner == rank) & (line < MINE) & (over == h * MINE + line)
        lay_ref[cut] = jnp.where(lay, 1.0, 0.0)
        lay = (owner == (rank + 1) % RANKS) & (line == 0) & (over == 0)
        mark_ref[cut] = jnp.where(lay, 1.0, 0.0)


def project(*refs):
    sources, (part_ref, fixed_ref, *told), held, sems = refs[:8], refs[8:14], refs[14:22], refs[22]
    act, grad, pin, pout, lengths, owners, sets, val = held
    moves = [(sources[i], held[i]) for i in (4, 5, 6, 7, 3, 1, 2)]
    cuts = [pl.ds(lo, hi - lo) for lo, hi in zip(CUTS[:-1], CUTS[1:])]
    moves += [(sources[0].at[:, cut], act.at[:, cut]) for cut in cuts]
    copies = [pltpu.make_async_copy(*move, sems.at[i]) for i, move in enumerate(moves)]
    for copy in copies:
        copy.start()
    fix(fixed_ref)
    for copy in copies[:4]:
        copy.wait()
    tell(lengths, owners, sets, val, *told)
    copies[4].wait()
    copies[5].wait()
    out = lax.dot_general(pout[...], grad[...], NT, preferred_element_type=f32)
    copies[6].wait()
    total = None
    for cut, copy in zip(cuts, copies[7:]):
        copy.wait()
        term = lax.dot_general(pin[:, cut], act[:, cut], NT, preferred_element_type=f32)
        total = term if total is None else total + term
    tokens = MINE * SLOTS
    for j in range(RANKS):
        cut = slice(j * tokens, (j + 1) * tokens)
        part_ref[j] = jnp.concatenate([total[:, cut], out[:, cut]], 1).astype(bf16)


def gradients(part_ref, live_ref, base_ref, out_ref, square):
    whole = jnp.sum(part_ref[...].astype(f32), 0)
    turned = pltpu.roll(whole, MINE * SLOTS, 1)
    turned = jnp.where(live_ref[...] > 0.0, jnp.concatenate([turned] * MINE, 0), 0.0)
    square[...] = lax.dot_general(
        turned, whole, NT, precision=lax.Precision.HIGHEST, preferred_element_type=f32
    )
    step = WIDTH // RANKS
    flat = []
    for q in range(MINE):
        lines = [square[pl.ds(q * WIDTH + r, RANKS, stride=step), :] for r in range(step)]
        flat.append(jnp.concatenate(lines, 1))
    shape = (RANKS, 8, FEATS)
    flat = [jnp.broadcast_to(line[:, None, :], shape) for line in flat]
    flat = jnp.where(iota(shape, 1) == 0, flat[0], flat[1])
    for h in range(HALVES):
        cut = pl.ds(h * RANKS, RANKS)
        out_ref[cut] = jnp.concatenate([flat, base_ref[cut]], 2)[:, :MINE].astype(bf16)


def pack(got_ref, lay_ref, mark_ref, out_ref):
    x = got_ref[...].astype(f32)
    x = jnp.concatenate([x, jnp.zeros((x.shape[0], 8 - MINE, LINE), f32)], 1)
    shape = x.shape[:2] + (128,)
    slot = jnp.broadcast_to(x[:, :, FEATS + SLOT : FEATS + SLOT + 1], shape).astype(i32)
    moves = jnp.where((iota(shape, 1) < MINE) & (slot == iota(shape, 2)), 1.0, 0.0)
    moves, lay, mark = (m.reshape(-1, 128).astype(bf16) for m in (moves, lay_ref[...], mark_ref[...]))
    x = x.reshape(-1, LINE).astype(bf16)
    own = jnp.concatenate([x[:, :FEATS], x[:, 3 * FEATS :]], 1)
    own = lax.dot_general(moves, own, TN, preferred_element_type=f32)
    val = lax.dot_general(lay, x[:, FEATS : 3 * FEATS], TN, preferred_element_type=f32)
    marks = lax.dot_general(mark, x[:, FEATS : FEATS + 128], TN, preferred_element_type=f32)
    out = jnp.concatenate([own[:, :FEATS], val, own[:, FEATS:] + marks], 1)
    out_ref[...] = out.reshape(DESTS, 8, LINE)[:, :LOT].astype(bf16)


def score(came_ref, fixed_ref, grads_ref, spread_ref, sets_ref):
    x = came_ref[...].astype(f32)
    x = jnp.concatenate([x, jnp.zeros(x.shape, f32)], 1).reshape(DESTS * 8, LINE)
    small = x[:, 3 * FEATS :]
    lane = iota(small.shape, 1)
    chooser = jnp.where(small.astype(i32) == lane + 1, 1.0, 0.0).astype(bf16)
    x = x.astype(bf16)
    source_grads = lax.dot_general(chooser, x[:, :FEATS], TN, preferred_element_type=f32)[:SRC_DEV]
    grads_ref[...] = source_grads
    marks = jnp.dot(small.astype(bf16), fixed_ref[:, 256:384], preferred_element_type=f32)
    marks = jnp.sum(marks * fixed_ref[:, 384:].astype(f32), 0, keepdims=True)
    sets_ref[...] = jnp.broadcast_to(marks, sets_ref.shape)
    val = jnp.concatenate([x[:, FEATS : 2 * FEATS], x[:, 2 * FEATS : 3 * FEATS]], 0)
    val = jnp.dot(fixed_ref[:, :256], val, preferred_element_type=f32)
    pair = lax.dot_general(source_grads, val, NT, precision=lax.Precision.HIGHEST, preferred_element_type=f32)
    spread_ref[...] = jnp.broadcast_to(pair[None], spread_ref.shape)


def finish(parts_ref, sets_ref, grads_ref, pair_ref, set_ref, out_ref):
    out_ref[...] = grads_ref[...]
    pair = jnp.sum(parts_ref[...], 0)
    pair_ref[...] = pair
    hot = jnp.where(sets_ref[...].astype(i32) == iota(sets_ref.shape, 0) + 1, 1.0, 0.0)
    total = lax.dot_general(hot, pair, NT, precision=lax.Precision.HIGHEST, preferred_element_type=f32)
    set_ref[...] = (total / jnp.sum(hot, 1, keepdims=True))[:SETS]


VMEM = pl.BlockSpec(memory_space=pltpu.VMEM)
HBM = pl.BlockSpec(memory_space=pltpu.HBM)
PARAMS = pltpu.CompilerParams(vmem_limit_bytes=32 * 2**20)


def here(x):
    return pltpu.with_memory_space_constraint(x, pltpu.VMEM)


def far(x):
    return pltpu.with_memory_space_constraint(x, pltpu.HBM)


def call(kernel, out, specs, scratch=(), **kw):
    return pl.pallas_call(
        kernel,
        out_shape=out,
        in_specs=specs,
        out_specs=jax.tree.map(lambda _: VMEM, out),
        scratch_shapes=scratch,
        compiler_params=PARAMS,
        **kw,
    )


def exchange(blocks, axes):
    return lax.all_to_all(blocks, axes, 0, 0, tiled=True)


def local(act_in, grad_out, proj_in, proj_out, lengths, sources, val_feats, val_sets):
    chunks = HALVES * RANKS
    args = (act_in, grad_out, proj_in.T, proj_out.T, lengths, sources, val_sets.T, val_feats)
    homes = [pltpu.VMEM] * 4 + [pltpu.SMEM] * 3 + [pltpu.VMEM]
    part, fixed, live, base, lay, mark = call(
        project,
        [
            pltpu.VMEM((RANKS, WIDTH, 2 * MINE * SLOTS), bf16),
            pltpu.VMEM((NVAL, 512), bf16),
            pltpu.VMEM((MINE * WIDTH, 2 * WIDTH), f32),
            pltpu.VMEM((chunks, 8, REST), f32),
            pltpu.VMEM((chunks, 8, 128), f32),
            pltpu.VMEM((chunks, 8, 128), f32),
        ],
        [HBM] * 8,
        [home(x.shape, x.dtype) for home, x in zip(homes, args)] + [pltpu.SemaphoreType.DMA((6 + len(CUTS),))],
    )(*(far(x) for x in args))
    part = exchange(part, TENSOR)
    block = call(gradients, pltpu.VMEM((chunks, MINE, LINE), bf16), [VMEM] * 3, [pltpu.VMEM((MINE * WIDTH, WIDTH), f32)])(
        here(part), here(live), here(base)
    )
    got = exchange(block, ("h",) + TENSOR)
    packed = call(pack, pltpu.VMEM((DESTS, LOT, LINE), bf16), [VMEM] * 3)(here(got), here(lay), here(mark))
    came = exchange(packed, ("y", "c"))
    source_grads, spread, sets = call(
        score,
        [
            pltpu.VMEM((SRC_DEV, FEATS), f32),
            pltpu.VMEM((RANKS, SRC_DEV, NVAL), f32),
            pltpu.VMEM((8, NVAL), f32),
        ],
        [VMEM] * 2,
    )(here(came), here(fixed))
    parts = exchange(spread, TENSOR)
    pair_scores, set_scores, source_grads = call(
        finish,
        [
            jax.ShapeDtypeStruct((SRC_DEV, NVAL), f32),
            jax.ShapeDtypeStruct((SETS, SRC_DEV), f32),
            jax.ShapeDtypeStruct((SRC_DEV, FEATS), f32),
        ],
        [VMEM] * 3,
    )(here(parts), here(sets), here(source_grads))
    return (source_grads, pair_scores, set_scores.T)


def solution(mesh):
    parts = Mesh(mesh.devices.reshape(SPLIT), NAMES)
    placed = (
        P(DP, TENSOR),
        P(DP, TENSOR),
        P(TENSOR, None),
        P(TENSOR, None),
        P(DP),
        P(DP),
        P(DP, TENSOR),
        P(DP, None),
    )
    return jax.shard_map(
        local,
        mesh=parts,
        in_specs=placed,
        out_specs=(P(DP, TENSOR), P(DP, None), P(DP, None)),
        check_vma=False,
    )
```

```python
import jax
import jax.numpy as jnp
from jax import lax
from jax.experimental import pallas as pl
from jax.experimental.pallas import tpu as pltpu
from jax.sharding import Mesh, PartitionSpec as P

SETS = 4
SRC_DEV = 8
SPLIT = (8, 2, 2, 4, 4)
NAMES = ("y", "h", "c", "z", "x")
DP = ("y", "h", "c")
TENSOR = ("z", "x")
HALVES, CORES, RANKS = 2, 2, 16
DESTS = 16
SEQS, SLOTS, WIDTH = 32, 32, 64
MINE = SEQS // RANKS
FEATS = WIDTH * WIDTH // RANKS
VALS = 4
NVAL = 128
CAP = 2
LOT = HALVES * CAP
LINE = 3 * FEATS + 128
REST = LINE - FEATS
MARK = 8
SLOT = 2 * FEATS + 64
NONE = 256.0
CUTS = (0, 256, 512, 1024, 1536, 1792)
bf16, f32, i32 = jnp.bfloat16, jnp.float32, jnp.int32
NT = (((1,), (1,)), ((), ()))
TN = (((0,), (0,)), ((), ()))


def iota(shape, dim):
    return lax.broadcasted_iota(i32, shape, dim)


def tell(lengths, sources, sets, val, live_ref, base_ref, lay_ref, mark_ref):
    rank, half = lax.axis_index(TENSOR), lax.axis_index("h")
    for q in range(MINE):
        slot = iota((WIDTH, 2 * WIDTH), 1) - q * SLOTS
        live_ref[q] = jnp.where((slot >= 0) & (slot < lengths[rank * MINE + q]), 1.0, 0.0)
    lane = iota((1, REST), 1)
    marks = jnp.zeros((1, REST), f32)
    for r in range(VALS):
        marks = jnp.where(lane == MARK + half * VALS + r, (sets[0, r] + 1).astype(f32), marks)
    told = []
    for q in range(MINE):
        s = rank * MINE + q
        source = sources[s]
        owner = source // SRC_DEV
        order = jnp.int32(0)
        for other in range(SEQS):
            same = (sources[other] // SRC_DEV == owner) & (other < s)
            order = order + same.astype(i32)
        dest = owner // (HALVES * CORES) * CORES + owner % CORES
        told.append((owner // CORES % HALVES, dest * 8 + half * CAP + order, source % SRC_DEV + 1))
    shape = (RANKS, 8, REST)
    row, chunk = iota(shape, 1), iota(shape, 0)
    base_ref[0] = jnp.zeros((8, REST), f32)
    rows = val[...].astype(f32)
    for r in range(VALS):
        base_ref[0, r // 2 : r // 2 + 1, r % 2 * FEATS : (r % 2 + 1) * FEATS] = rows[r : r + 1]
    rows = jnp.broadcast_to(base_ref[0][None], shape)
    rows = jnp.where(chunk == rank, rows, jnp.where(row == 0, jnp.broadcast_to(marks[None], shape), 0.0))
    small = (RANKS, 8, 128)
    line, over, owner = iota(small, 1), iota(small, 2) % 8, iota(small, 0)
    for h in range(HALVES):
        cut = pl.ds(h * RANKS, RANKS)
        sent = rows
        for q in range(MINE):
            to, slot, tag = told[q]
            slot = jnp.where(to == h, slot, jnp.int32(NONE)).astype(f32)
            word = jnp.where(lane >= SLOT, slot, jnp.where(lane < 2 * FEATS + MARK, tag.astype(f32), 0.0))
            sent = jnp.where((row == q) & (iota(shape, 2) >= 2 * FEATS), jnp.broadcast_to(word[None], shape), sent)
        base_ref[cut] = sent
        lay = (owner == rank) & (line < MINE) & (over == h * MINE + line)
        lay_ref[cut] = jnp.where(lay, 1.0, 0.0)
        lay = (owner == (rank + 1) % RANKS) & (line == 0) & (over == 0)
        mark_ref[cut] = jnp.where(lay, 1.0, 0.0)


def project(*refs):
    sources, (part_ref, *told), held, sems = refs[:8], refs[8:13], refs[13:21], refs[21]
    act, grad, pin, pout, lengths, owners, sets, val = held
    moves = [(sources[i], held[i]) for i in (4, 5, 6, 7, 3, 1, 2)]
    cuts = [pl.ds(lo, hi - lo) for lo, hi in zip(CUTS[:-1], CUTS[1:])]
    moves += [(sources[0].at[:, cut], act.at[:, cut]) for cut in cuts]
    copies = [pltpu.make_async_copy(*move, sems.at[i]) for i, move in enumerate(moves)]
    for copy in copies:
        copy.start()
    for copy in copies[:4]:
        copy.wait()
    tell(lengths, owners, sets, val, *told)
    copies[4].wait()
    copies[5].wait()
    out = lax.dot_general(pout[...], grad[...], NT, preferred_element_type=f32)
    copies[6].wait()
    total = None
    for cut, copy in zip(cuts, copies[7:]):
        copy.wait()
        term = lax.dot_general(pin[:, cut], act[:, cut], NT, preferred_element_type=f32)
        total = term if total is None else total + term
    tokens = MINE * SLOTS
    for j in range(RANKS):
        cut = slice(j * tokens, (j + 1) * tokens)
        part_ref[j] = jnp.concatenate([total[:, cut], out[:, cut]], 1).astype(bf16)


def gradients(part_ref, live_ref, base_ref, out_ref, square):
    whole = jnp.sum(part_ref[...].astype(f32), 0)
    turned = pltpu.roll(whole, MINE * SLOTS, 1)
    flat = []
    for q in range(MINE):
        square[q] = lax.dot_general(
            jnp.where(live_ref[q] > 0.0, turned, 0.0),
            whole,
            NT,
            precision=lax.Precision.HIGHEST,
            preferred_element_type=f32,
        )
        step = WIDTH // RANKS
        lines = [square[q, pl.ds(r, RANKS, stride=step), :] for r in range(step)]
        flat.append(jnp.concatenate(lines, 1))
    shape = (RANKS, 8, FEATS)
    flat = [jnp.broadcast_to(line[:, None, :], shape) for line in flat]
    flat = jnp.where(iota(shape, 1) == 0, flat[0], flat[1])
    for h in range(HALVES):
        cut = pl.ds(h * RANKS, RANKS)
        out_ref[cut] = jnp.concatenate([flat, base_ref[cut]], 2)[:, :MINE].astype(bf16)


def pack(got_ref, lay_ref, mark_ref, out_ref):
    x = got_ref[...].astype(f32)
    x = jnp.concatenate([x, jnp.zeros((x.shape[0], 8 - MINE, LINE), f32)], 1)
    shape = x.shape[:2] + (128,)
    slot = jnp.broadcast_to(x[:, :, FEATS + SLOT : FEATS + SLOT + 1], shape).astype(i32)
    moves = jnp.where((iota(shape, 1) < MINE) & (slot == iota(shape, 2)), 1.0, 0.0)
    moves, lay, mark = (m.reshape(-1, 128).astype(bf16) for m in (moves, lay_ref[...], mark_ref[...]))
    x = x.reshape(-1, LINE).astype(bf16)
    own = jnp.concatenate([x[:, :FEATS], x[:, 3 * FEATS :]], 1)
    own = lax.dot_general(moves, own, TN, preferred_element_type=f32)
    val = lax.dot_general(lay, x[:, FEATS : 3 * FEATS], TN, preferred_element_type=f32)
    marks = lax.dot_general(mark, x[:, FEATS : FEATS + 128], TN, preferred_element_type=f32)
    out = jnp.concatenate([own[:, :FEATS], val, own[:, FEATS:] + marks], 1)
    out_ref[...] = out.reshape(DESTS, 8, LINE)[:, :LOT].astype(bf16)


def score(came_ref, grads_ref, spread_ref, sets_ref):
    x = came_ref[...].astype(f32)
    x = jnp.concatenate([x, jnp.zeros(x.shape, f32)], 1).reshape(DESTS * 8, LINE)
    small = x[:, 3 * FEATS :]
    n, lane = iota(small.shape, 0), iota(small.shape, 1)
    chooser = jnp.where(small.astype(i32) == lane + 1, 1.0, 0.0).astype(bf16)
    x = x.astype(bf16)
    source_grads = lax.dot_general(chooser, x[:, :FEATS], TN, preferred_element_type=f32)[:SRC_DEV]
    grads_ref[...] = source_grads

    def parts(v):
        return v % VALS, v // VALS % CORES, v // (VALS * CORES) % HALVES, v // (VALS * CORES * HALVES)

    r, c, h, y = parts(lane)
    spread = jnp.where(n == MARK + h * VALS + r, 1.0, 0.0).astype(bf16)
    marks = jnp.dot(small.astype(bf16), spread, preferred_element_type=f32)
    marks = jnp.sum(jnp.where(n == (y * CORES + c) * 8, marks, 0.0), 0, keepdims=True)
    sets_ref[...] = jnp.broadcast_to(marks, sets_ref.shape)
    shape = (NVAL, 2 * DESTS * 8)
    r, c, h, y = parts(iota(shape, 0))
    pick = iota(shape, 1) == r % 2 * (DESTS * 8) + (y * CORES + c) * 8 + (h * VALS + r) // 2
    val = jnp.concatenate([x[:, FEATS : 2 * FEATS], x[:, 2 * FEATS : 3 * FEATS]], 0)
    val = jnp.dot(jnp.where(pick, 1.0, 0.0).astype(bf16), val, preferred_element_type=f32)
    pair = lax.dot_general(source_grads, val, NT, precision=lax.Precision.HIGHEST, preferred_element_type=f32)
    spread_ref[...] = jnp.broadcast_to(pair[None], spread_ref.shape)


def finish(parts_ref, sets_ref, grads_ref, pair_ref, set_ref, out_ref):
    out_ref[...] = grads_ref[...]
    pair = jnp.sum(parts_ref[...], 0)
    pair_ref[...] = pair
    hot = jnp.where(sets_ref[...].astype(i32) == iota(sets_ref.shape, 0) + 1, 1.0, 0.0)
    total = lax.dot_general(hot, pair, NT, precision=lax.Precision.HIGHEST, preferred_element_type=f32)
    set_ref[...] = (total / jnp.sum(hot, 1, keepdims=True))[:SETS]


VMEM = pl.BlockSpec(memory_space=pltpu.VMEM)
HBM = pl.BlockSpec(memory_space=pltpu.HBM)
PARAMS = pltpu.CompilerParams(vmem_limit_bytes=32 * 2**20)


def here(x):
    return pltpu.with_memory_space_constraint(x, pltpu.VMEM)


def far(x):
    return pltpu.with_memory_space_constraint(x, pltpu.HBM)


def call(kernel, out, specs, scratch=(), **kw):
    return pl.pallas_call(
        kernel,
        out_shape=out,
        in_specs=specs,
        out_specs=jax.tree.map(lambda _: VMEM, out),
        scratch_shapes=scratch,
        compiler_params=PARAMS,
        **kw,
    )


def exchange(blocks, axes):
    return lax.all_to_all(blocks, axes, 0, 0, tiled=True)


def local(act_in, grad_out, proj_in, proj_out, lengths, sources, val_feats, val_sets):
    chunks = HALVES * RANKS
    args = (act_in, grad_out, proj_in.T, proj_out.T, lengths, sources, val_sets.T, val_feats)
    homes = [pltpu.VMEM] * 4 + [pltpu.SMEM] * 3 + [pltpu.VMEM]
    part, live, base, lay, mark = call(
        project,
        [
            pltpu.VMEM((RANKS, WIDTH, 2 * MINE * SLOTS), bf16),
            pltpu.VMEM((MINE, WIDTH, 2 * WIDTH), f32),
            pltpu.VMEM((chunks, 8, REST), f32),
            pltpu.VMEM((chunks, 8, 128), f32),
            pltpu.VMEM((chunks, 8, 128), f32),
        ],
        [HBM] * 8,
        [home(x.shape, x.dtype) for home, x in zip(homes, args)] + [pltpu.SemaphoreType.DMA((6 + len(CUTS),))],
    )(*(far(x) for x in args))
    part = exchange(part, TENSOR)
    block = call(gradients, pltpu.VMEM((chunks, MINE, LINE), bf16), [VMEM] * 3, [pltpu.VMEM((MINE, WIDTH, WIDTH), f32)])(
        here(part), here(live), here(base)
    )
    got = exchange(block, ("h",) + TENSOR)
    packed = call(pack, pltpu.VMEM((DESTS, LOT, LINE), bf16), [VMEM] * 3)(here(got), here(lay), here(mark))
    came = exchange(packed, ("y", "c"))
    source_grads, spread, sets = call(
        score,
        [
            pltpu.VMEM((SRC_DEV, FEATS), f32),
            pltpu.VMEM((RANKS, SRC_DEV, NVAL), f32),
            pltpu.VMEM((8, NVAL), f32),
        ],
        [VMEM],
    )(here(came))
    parts = exchange(spread, ("x", "z"))
    pair_scores, set_scores, source_grads = call(
        finish,
        [
            jax.ShapeDtypeStruct((SRC_DEV, NVAL), f32),
            jax.ShapeDtypeStruct((SETS, SRC_DEV), f32),
            jax.ShapeDtypeStruct((SRC_DEV, FEATS), f32),
        ],
        [VMEM] * 3,
    )(here(parts), here(sets), here(source_grads))
    return (source_grads, pair_scores, set_scores.T)


def solution(mesh):
    parts = Mesh(mesh.devices.reshape(SPLIT), NAMES)
    placed = (
        P(DP, TENSOR),
        P(DP, TENSOR),
        P(TENSOR, None),
        P(TENSOR, None),
        P(DP),
        P(DP),
        P(DP, TENSOR),
        P(DP, None),
    )
    return jax.shard_map(
        local,
        mesh=parts,
        in_specs=placed,
        out_specs=(P(DP, TENSOR), P(DP, None), P(DP, None)),
        check_vma=False,
    )
```

```python
import jax
import jax.numpy as jnp
from jax import lax
from jax.experimental import pallas as pl
from jax.experimental.pallas import tpu as pltpu
from jax.sharding import Mesh, PartitionSpec as P

SETS = 4
SRC_DEV = 8
SPLIT = (8, 2, 2, 4, 4)
NAMES = ("y", "h", "c", "z", "x")
DP = ("y", "h", "c")
TENSOR = ("z", "x")
HALVES, CORES, RANKS = 2, 2, 16
DESTS = 16
SEQS, SLOTS, WIDTH = 32, 32, 64
MINE = SEQS // RANKS
FEATS = WIDTH * WIDTH // RANKS
VALS = 4
NVAL = 128
CAP = 2
LOT = HALVES * CAP
LINE = 3 * FEATS + 128
REST = LINE - FEATS
MARK = 8
SLOT = 2 * FEATS + 64
NONE = 256.0
CUTS = (0, 256, 512, 1024, 1536, 1792)
bf16, f32, i32 = jnp.bfloat16, jnp.float32, jnp.int32
NT = (((1,), (1,)), ((), ()))
TN = (((0,), (0,)), ((), ()))


def iota(shape, dim):
    return lax.broadcasted_iota(i32, shape, dim)


def parts(v):
    return v % VALS, v // VALS % CORES, v // (VALS * CORES) % HALVES, v // (VALS * CORES * HALVES)


def fix(fixed_ref):
    shape = (NVAL, 2 * DESTS * 8)
    r, c, h, y = parts(iota(shape, 0))
    pick = iota(shape, 1) == r % 2 * (DESTS * 8) + (y * CORES + c) * 8 + (h * VALS + r) // 2
    fixed_ref[:, :256] = jnp.where(pick, 1.0, 0.0).astype(bf16)
    n, v = iota((128, NVAL), 0), iota((128, NVAL), 1)
    r, c, h, y = parts(v)
    fixed_ref[:, 256:384] = jnp.where(n == MARK + h * VALS + r, 1.0, 0.0).astype(bf16)
    fixed_ref[:, 384:] = jnp.where(n == (y * CORES + c) * 8, 1.0, 0.0).astype(bf16)


def tell(lengths, sources, sets, val, live_ref, base_ref, lay_ref, mark_ref):
    rank, half = lax.axis_index(TENSOR), lax.axis_index("h")
    for q in range(MINE):
        slot = iota((WIDTH, 2 * WIDTH), 1) - q * SLOTS
        live_ref[q * WIDTH : (q + 1) * WIDTH, :] = jnp.where((slot >= 0) & (slot < lengths[rank * MINE + q]), 1.0, 0.0)
    lane = iota((1, REST), 1)
    marks = jnp.zeros((1, REST), f32)
    for r in range(VALS):
        marks = jnp.where(lane == MARK + half * VALS + r, (sets[0, r] + 1).astype(f32), marks)
    told = []
    for q in range(MINE):
        s = rank * MINE + q
        source = sources[s]
        owner = source // SRC_DEV
        order = jnp.int32(0)
        for other in range(SEQS):
            same = (sources[other] // SRC_DEV == owner) & (other < s)
            order = order + same.astype(i32)
        dest = owner // (HALVES * CORES) * CORES + owner % CORES
        told.append((owner // CORES % HALVES, dest * 8 + half * CAP + order, source % SRC_DEV + 1))
    shape = (RANKS, 8, REST)
    row, chunk = iota(shape, 1), iota(shape, 0)
    base_ref[0] = jnp.zeros((8, REST), f32)
    rows = val[...].astype(f32)
    for r in range(VALS):
        base_ref[0, r // 2 : r // 2 + 1, r % 2 * FEATS : (r % 2 + 1) * FEATS] = rows[r : r + 1]
    rows = jnp.broadcast_to(base_ref[0][None], shape)
    rows = jnp.where(chunk == rank, rows, jnp.where(row == 0, jnp.broadcast_to(marks[None], shape), 0.0))
    small = (RANKS, 8, 128)
    line, over, owner = iota(small, 1), iota(small, 2) % 8, iota(small, 0)
    for h in range(HALVES):
        cut = pl.ds(h * RANKS, RANKS)
        sent = rows
        for q in range(MINE):
            to, slot, tag = told[q]
            slot = jnp.where(to == h, slot, jnp.int32(NONE)).astype(f32)
            word = jnp.where(lane >= SLOT, slot, jnp.where(lane < 2 * FEATS + MARK, tag.astype(f32), 0.0))
            sent = jnp.where((row == q) & (iota(shape, 2) >= 2 * FEATS), jnp.broadcast_to(word[None], shape), sent)
        base_ref[cut] = sent
        lay = (owner == rank) & (line < MINE) & (over == h * MINE + line)
        lay_ref[cut] = jnp.where(lay, 1.0, 0.0)
        lay = (owner == (rank + 1) % RANKS) & (line == 0) & (over == 0)
        mark_ref[cut] = jnp.where(lay, 1.0, 0.0)


def project(*refs):
    sources, (part_ref, fixed_ref, *told), held, sems = refs[:8], refs[8:14], refs[14:22], refs[22]
    act, grad, pin, pout, lengths, owners, sets, val = held
    moves = [(sources[i], held[i]) for i in (4, 5, 6, 7, 3, 1, 2)]
    cuts = [pl.ds(lo, hi - lo) for lo, hi in zip(CUTS[:-1], CUTS[1:])]
    moves += [(sources[0].at[:, cut], act.at[:, cut]) for cut in cuts]
    copies = [pltpu.make_async_copy(*move, sems.at[i]) for i, move in enumerate(moves)]
    for copy in copies:
        copy.start()
    fix(fixed_ref)
    for copy in copies[:4]:
        copy.wait()
    tell(lengths, owners, sets, val, *told)
    copies[4].wait()
    copies[5].wait()
    out = lax.dot_general(pout[...], grad[...], NT, preferred_element_type=f32)
    copies[6].wait()
    total = None
    for cut, copy in zip(cuts, copies[7:]):
        copy.wait()
        term = lax.dot_general(pin[:, cut], act[:, cut], NT, preferred_element_type=f32)
        total = term if total is None else total + term
    tokens = MINE * SLOTS
    for j in range(RANKS):
        cut = slice(j * tokens, (j + 1) * tokens)
        part_ref[j] = jnp.concatenate([total[:, cut], out[:, cut]], 1).astype(bf16)


def gradients(part_ref, live_ref, base_ref, out_ref, square):
    whole = jnp.sum(part_ref[...].astype(f32), 0)
    turned = pltpu.roll(whole, MINE * SLOTS, 1)
    turned = jnp.where(live_ref[...] > 0.0, jnp.concatenate([turned] * MINE, 0), 0.0)
    square[...] = lax.dot_general(
        turned, whole, NT, precision=lax.Precision.HIGHEST, preferred_element_type=f32
    )
    step = WIDTH // RANKS
    flat = []
    for q in range(MINE):
        lines = [square[pl.ds(q * WIDTH + r, RANKS, stride=step), :] for r in range(step)]
        flat.append(jnp.concatenate(lines, 1))
    shape = (RANKS, 8, FEATS)
    flat = [jnp.broadcast_to(line[:, None, :], shape) for line in flat]
    flat = jnp.where(iota(shape, 1) == 0, flat[0], flat[1])
    for h in range(HALVES):
        cut = pl.ds(h * RANKS, RANKS)
        out_ref[cut] = jnp.concatenate([flat, base_ref[cut]], 2)[:, :MINE].astype(bf16)


def pack(got_ref, lay_ref, mark_ref, out_ref):
    x = got_ref[...].astype(f32)
    x = jnp.concatenate([x, jnp.zeros((x.shape[0], 8 - MINE, LINE), f32)], 1)
    shape = x.shape[:2] + (128,)
    slot = jnp.broadcast_to(x[:, :, FEATS + SLOT : FEATS + SLOT + 1], shape).astype(i32)
    moves = jnp.where((iota(shape, 1) < MINE) & (slot == iota(shape, 2)), 1.0, 0.0)
    moves, lay, mark = (m.reshape(-1, 128).astype(bf16) for m in (moves, lay_ref[...], mark_ref[...]))
    x = x.reshape(-1, LINE).astype(bf16)
    own = jnp.concatenate([x[:, :FEATS], x[:, 3 * FEATS :]], 1)
    own = lax.dot_general(moves, own, TN, preferred_element_type=f32)
    val = lax.dot_general(lay, x[:, FEATS : 3 * FEATS], TN, preferred_element_type=f32)
    marks = lax.dot_general(mark, x[:, FEATS : FEATS + 128], TN, preferred_element_type=f32)
    out = jnp.concatenate([own[:, :FEATS], val, own[:, FEATS:] + marks], 1)
    out_ref[...] = out.reshape(DESTS, 8, LINE)[:, :LOT].astype(bf16)


def score(came_ref, fixed_ref, grads_ref, spread_ref, sets_ref):
    x = came_ref[...].astype(f32)
    x = jnp.concatenate([x, jnp.zeros(x.shape, f32)], 1).reshape(DESTS * 8, LINE)
    small = x[:, 3 * FEATS :]
    lane = iota(small.shape, 1)
    chooser = jnp.where(small.astype(i32) == lane + 1, 1.0, 0.0).astype(bf16)
    x = x.astype(bf16)
    source_grads = lax.dot_general(chooser, x[:, :FEATS], TN, preferred_element_type=f32)[:SRC_DEV]
    grads_ref[...] = source_grads
    marks = jnp.dot(small.astype(bf16), fixed_ref[:, 256:384], preferred_element_type=f32)
    marks = jnp.sum(marks * fixed_ref[:, 384:].astype(f32), 0, keepdims=True)
    sets_ref[...] = jnp.broadcast_to(marks, sets_ref.shape)
    val = jnp.concatenate([x[:, FEATS : 2 * FEATS], x[:, 2 * FEATS : 3 * FEATS]], 0)
    val = jnp.dot(fixed_ref[:, :256], val, preferred_element_type=f32)
    pair = lax.dot_general(source_grads, val, NT, precision=lax.Precision.HIGHEST, preferred_element_type=f32)
    spread_ref[...] = jnp.broadcast_to(pair[None], spread_ref.shape)


def finish(parts_ref, sets_ref, grads_ref, pair_ref, set_ref, out_ref):
    out_ref[...] = grads_ref[...]
    pair = jnp.sum(parts_ref[...], 0)
    pair_ref[...] = pair
    hot = jnp.where(sets_ref[...].astype(i32) == iota(sets_ref.shape, 0) + 1, 1.0, 0.0)
    total = lax.dot_general(hot, pair, NT, precision=lax.Precision.HIGHEST, preferred_element_type=f32)
    set_ref[...] = (total / jnp.sum(hot, 1, keepdims=True))[:SETS]


VMEM = pl.BlockSpec(memory_space=pltpu.VMEM)
HBM = pl.BlockSpec(memory_space=pltpu.HBM)
PARAMS = pltpu.CompilerParams(vmem_limit_bytes=32 * 2**20)


def here(x):
    return pltpu.with_memory_space_constraint(x, pltpu.VMEM)


def far(x):
    return pltpu.with_memory_space_constraint(x, pltpu.HBM)


def call(kernel, out, specs, scratch=(), **kw):
    return pl.pallas_call(
        kernel,
        out_shape=out,
        in_specs=specs,
        out_specs=jax.tree.map(lambda _: VMEM, out),
        scratch_shapes=scratch,
        compiler_params=PARAMS,
        **kw,
    )


def exchange(blocks, axes):
    return lax.all_to_all(blocks, axes, 0, 0, tiled=True)


def local(act_in, grad_out, proj_in, proj_out, lengths, sources, val_feats, val_sets):
    chunks = HALVES * RANKS
    args = (act_in, grad_out, proj_in.T, proj_out.T, lengths, sources, val_sets.T, val_feats)
    homes = [pltpu.VMEM] * 4 + [pltpu.SMEM] * 3 + [pltpu.VMEM]
    part, fixed, live, base, lay, mark = call(
        project,
        [
            pltpu.VMEM((RANKS, WIDTH, 2 * MINE * SLOTS), bf16),
            pltpu.VMEM((NVAL, 512), bf16),
            pltpu.VMEM((MINE * WIDTH, 2 * WIDTH), f32),
            pltpu.VMEM((chunks, 8, REST), f32),
            pltpu.VMEM((chunks, 8, 128), f32),
            pltpu.VMEM((chunks, 8, 128), f32),
        ],
        [HBM] * 8,
        [home(x.shape, x.dtype) for home, x in zip(homes, args)] + [pltpu.SemaphoreType.DMA((6 + len(CUTS),))],
    )(*(far(x) for x in args))
    part = exchange(part, TENSOR)
    block = call(gradients, pltpu.VMEM((chunks, MINE, LINE), bf16), [VMEM] * 3, [pltpu.VMEM((MINE * WIDTH, WIDTH), f32)])(
        here(part), here(live), here(base)
    )
    got = exchange(block, ("h",) + TENSOR)
    packed = call(pack, pltpu.VMEM((DESTS, LOT, LINE), bf16), [VMEM] * 3)(here(got), here(lay), here(mark))
    came = exchange(packed, ("y", "c"))
    source_grads, spread, sets = call(
        score,
        [
            pltpu.VMEM((SRC_DEV, FEATS), f32),
            pltpu.VMEM((RANKS, SRC_DEV, NVAL), f32),
            pltpu.VMEM((8, NVAL), f32),
        ],
        [VMEM] * 2,
    )(here(came), here(fixed))
    parts = exchange(spread, ("x", "z"))
    pair_scores, set_scores, source_grads = call(
        finish,
        [
            jax.ShapeDtypeStruct((SRC_DEV, NVAL), f32),
            jax.ShapeDtypeStruct((SETS, SRC_DEV), f32),
            jax.ShapeDtypeStruct((SRC_DEV, FEATS), f32),
        ],
        [VMEM] * 3,
    )(here(parts), here(sets), here(source_grads))
    return (source_grads, pair_scores, set_scores.T)


def solution(mesh):
    parts = Mesh(mesh.devices.reshape(SPLIT), NAMES)
    placed = (
        P(DP, TENSOR),
        P(DP, TENSOR),
        P(TENSOR, None),
        P(TENSOR, None),
        P(DP),
        P(DP),
        P(DP, TENSOR),
        P(DP, None),
    )
    return jax.shard_map(
        local,
        mesh=parts,
        in_specs=placed,
        out_specs=(P(DP, TENSOR), P(DP, None), P(DP, None)),
        check_vma=False,
    )
```
